512 devices in a mesh: grp: 32 (over y, x), mlp: 16 (over z, core).
Axes of the slice: x: 4, y: 8, z: 8, core: 2. Of those that a mesh axis runs over, the one named last changes fastest.
Arguments:
- queries: bfloat16 [32, 128, 4096], P('grp'), may hold values from -70 to 70
- fresh_kv: bfloat16 [32, 128, 1024], P('grp', 'mlp'), may hold values from -5 to 5
- kv_pages: bfloat16 [32, 32, 128, 1024], P('grp', 'mlp'), may hold values from -5 to 5
- residual: bfloat16 [32, 128, 4096], P('grp'), may hold values from -3 to 3
- norm_gain: float32 [4096], replicated, may hold values from 0.5 to 1.5
- out_weight: bfloat16 [4096, 4096], P('mlp', 'grp'), may hold values from -0.09375 to 0.09375
- gate_weight: bfloat16 [4096, 6144], P('grp', 'mlp'), may hold values from -0.09375 to 0.09375
- up_weight: bfloat16 [4096, 6144], P('grp', 'mlp'), may hold values from -0.09375 to 0.09375
- down_weight: bfloat16 [6144, 4096], P('mlp', 'grp'), may hold values from -0.078125 to 0.078125
- page_table: int32 [32, 16, 12], P('grp'), may hold values from -1 to 31, as said below
- shared_pages: int32 [32, 4], P('grp'), may hold values from 0 to 31, as said below
- cache_lens: int32 [32, 16], P('grp'), may hold values from 513 to 2048, as said below
- prefill_offsets: int32 [32], P('grp'), may hold values from 1 to 512
Outputs:
- layer_out: bfloat16 [32, 128, 4096], P('grp', 'mlp')
The draws below stay inside these ranges and needn't reach their ends.
Inputs may be any that keep to these rules, and one draw needn't show every extreme that they name: `page_table`: row d lists the pool pages that hold decode d's tokens after the shared prompt, in order, and -1 after its last page; no page appears twice in a group, and none is also a shared page. `shared_pages`: the pool pages of the group's shared prompt in order; they are the first 4 pages of every request of the group. `cache_lens`: decode d's cached tokens fill exactly its listed pages after the 4 shared pages; in every group one decode has the most.
All inputs are finite; a program needn't handle non-finite values.
Results may differ from the reference program's by a relative error of at most 0.029.
Values may be sent and summed in bfloat16 or wider, within the bound.
No kernel may reach another device: no remote copies, remote signals or barrier semaphores. Data moves between devices by JAX's collectives and lax.ppermute only.
A program may use at most 128 MiB of HBM per device.

```python
import jax
import jax.numpy as jnp
from jax import lax

D = 4096
HEADS = 32
KV_HEADS = 4
HEAD = 128
FF = 6144
PAGE = 128
PAGES = 32
SHARED_PAGES = 4
PRIVATE_PAGES = 12
DECODES = 16
PREFILL = 112
ROWS = 128
GROUPS = 32
N_MLP = 16


def page_plan(key):
    folded = jax.random.fold_in(key, 7)

    def one_group(group_key):
        key_order, key_longest, key_counts, key_tail = jax.random.split(group_key, 4)
        page_order = jax.random.permutation(key_order, PAGES).astype(jnp.int32)
        longest = jax.random.randint(key_longest, (), 0, DECODES).astype(jnp.int32)
        spread = (PAGES - SHARED_PAGES - PRIVATE_PAGES) // (DECODES - 1)
        decode_ids = jnp.arange(DECODES, dtype=jnp.int32)
        counts = jax.random.randint(key_counts, (DECODES,), 1, spread + 1).astype(jnp.int32)
        counts = jnp.where(decode_ids == longest, PRIVATE_PAGES, counts).astype(jnp.int32)
        starts = SHARED_PAGES + jnp.cumsum(counts, dtype=jnp.int32) - counts
        column = jnp.arange(PRIVATE_PAGES, dtype=jnp.int32)
        position = jnp.minimum(starts[:, None] + column[None, :], PAGES - 1)
        page_rows = jnp.where(column[None, :] < counts[:, None], jnp.take(page_order, position), -1)
        tail_len = jax.random.randint(key_tail, (DECODES,), 1, PAGE + 1).astype(jnp.int32)
        lengths = (SHARED_PAGES + counts - 1) * PAGE + tail_len
        lengths = jnp.where(decode_ids == longest, (SHARED_PAGES + PRIVATE_PAGES) * PAGE, lengths)
        return (page_rows.astype(jnp.int32), page_order[:SHARED_PAGES], lengths.astype(jnp.int32))
    return jax.vmap(one_group)(jax.random.split(folded, GROUPS))


def token_plan(key):
    folded = jax.random.fold_in(key, 11)
    key_query, key_fresh = jax.random.split(folded)
    query_shape = (GROUPS, ROWS, HEADS * HEAD)
    fresh_shape = (GROUPS, ROWS, 2 * KV_HEADS * HEAD)
    query_draw = jnp.clip(3.0 * jax.random.normal(key_query, query_shape, jnp.float32), -15.0, 15.0)
    fresh_draw = jnp.clip(jax.random.normal(key_fresh, fresh_shape, jnp.float32), -5.0, 5.0)
    return (query_draw, fresh_draw)


def draw_queries(key, part):
    return token_plan(key)[0].astype(jnp.bfloat16)


def draw_fresh_kv(key, part):
    return token_plan(key)[1].astype(jnp.bfloat16)


def draw_page_table(key, part):
    return page_plan(key)[0]


def draw_shared_pages(key, part):
    return page_plan(key)[1]


def draw_cache_lens(key, part):
    return page_plan(key)[2]


def place_ends(result, rng, least, high):
    extent = result.shape
    place = [jax.random.randint(jax.random.fold_in(rng, axis), (), 0, extent[axis]) for axis in range(len(extent))]
    result = result.at[tuple(place)].set(least)
    longest = extent.index(max(extent))
    place[longest] = (place[longest] + 1) % extent[longest]
    return result.at[tuple(place)].set(high)


def shard_levels(own_key, shape, cuts, low, largest):
    def one(dim, shards_of):
        steps = jax.random.uniform(jax.random.fold_in(jax.random.fold_in(own_key, 6), dim), (shards_of,), jnp.float32, low / len(cuts), largest / len(cuts))
        return jnp.repeat(jnp.exp(steps), shape[dim] // shards_of).reshape((-1,) + (1,) * (len(shape) - dim - 1))

    loudness = one(*cuts[0])
    for cut in cuts[1:]:
        loudness = loudness * one(*cut)
    return loudness


def gaussian(stream_key, extent, deviation, most, shards=(), kind=jnp.bfloat16):
    drawn = jax.random.normal(stream_key, extent, jnp.float32) * deviation
    if len(shards) > 0:
        drawn = shard_levels(stream_key, extent, shards, -0.22, 0.18) * drawn
    return jnp.clip(drawn, min=-most, max=most).astype(kind)


def setup_inputs(seed: int = 0) -> dict:
    key_of = jax.random.split(jax.random.key(seed), 14)
    return {
        "queries": draw_queries(jax.random.fold_in(key_of[13], 71), 0),
        "fresh_kv": draw_fresh_kv(jax.random.fold_in(key_of[13], 71), 0),
        "kv_pages": gaussian(key_of[2], (GROUPS, PAGES, PAGE, 2 * KV_HEADS * HEAD), 1.0, 5.0, ((0, 32), (1, 16))),
        "residual": gaussian(key_of[3], (GROUPS, ROWS, D), 0.5, 3.0, ((0, 32),)),
        "norm_gain": jnp.clip(jax.random.uniform(key_of[4], (D,), jnp.float32, 0.5, 1.5), 0.5, 1.5),
        "out_weight": gaussian(key_of[5], (HEADS * HEAD, D), (HEADS * HEAD) ** -0.5, 0.09375, ((0, 16), (1, 32))),
        "gate_weight": gaussian(key_of[6], (D, FF), D ** -0.5, 0.09375, ((0, 32), (1, 16))),
        "up_weight": gaussian(key_of[7], (D, FF), D ** -0.5, 0.09375, ((0, 32), (1, 16))),
        "down_weight": gaussian(key_of[8], (FF, D), FF ** -0.5, 0.078125, ((0, 16), (1, 32))),
        "page_table": draw_page_table(jax.random.fold_in(key_of[13], 71), 0),
        "shared_pages": draw_shared_pages(jax.random.fold_in(key_of[13], 71), 0),
        "cache_lens": draw_cache_lens(jax.random.fold_in(key_of[13], 71), 0),
        "prefill_offsets": place_ends(jax.random.randint(key_of[12], (GROUPS,), 1, SHARED_PAGES * PAGE + 1), jax.random.fold_in(key_of[12], 1), 1, SHARED_PAGES * PAGE).astype(jnp.int32),
    }


NEG_FILL = -1e+30
EPSILON = 1e-05

def page_layout(page_ids, table_group, shared_group):
    shared_match = shared_group[None, :] == page_ids[:, None]
    is_shared = jnp.any(shared_match, axis=1)
    shared_slot = lax.optimization_barrier(jnp.sum(jnp.where(shared_match, jnp.arange(SHARED_PAGES, dtype=jnp.int32)[None, :], 0), axis=1, dtype=jnp.int32))
    own_match = table_group[None, :, :] == page_ids[:, None, None]
    owner_id = lax.optimization_barrier(jnp.sum(jnp.where(own_match, jnp.arange(DECODES, dtype=jnp.int32)[None, :, None] + 1, 0), axis=(1, 2), dtype=jnp.int32)) - 1
    own_slot = lax.optimization_barrier(jnp.sum(jnp.where(own_match, jnp.arange(PRIVATE_PAGES, dtype=jnp.int32)[None, None, :], 0), axis=(1, 2), dtype=jnp.int32))
    page_base = jnp.where(is_shared, shared_slot * PAGE, (SHARED_PAGES + own_slot) * PAGE)
    key_pos = (page_base[:, None] + jnp.arange(PAGE, dtype=jnp.int32)[None, :]).reshape(-1)
    key_shared = jnp.repeat(is_shared, PAGE)
    key_owner = jnp.repeat(jnp.where(is_shared, -1, owner_id), PAGE)
    return (key_pos, key_shared, key_owner)

def row_layout(lens_group, offset_value):
    row_ids = jnp.arange(ROWS, dtype=jnp.int32)
    is_prefill = row_ids < PREFILL
    decode_id = jnp.where(is_prefill, -2, row_ids - PREFILL)
    picked = decode_id[:, None] == jnp.arange(DECODES, dtype=jnp.int32)[None, :]
    decode_limit = lax.optimization_barrier(jnp.sum(jnp.where(picked, lens_group[None, :], 0), axis=1, dtype=jnp.int32))
    limit = jnp.where(is_prefill, offset_value, decode_limit)
    return (row_ids, is_prefill, decode_id, limit)

def cache_visible(key_pos, key_shared, key_owner, decode_id, limit):
    belongs = key_shared[None, :] | (key_owner[None, :] == decode_id[:, None])
    return belongs & (key_pos[None, :] < limit[:, None])

def fresh_visible(key_rows, row_ids, is_prefill):
    before = (key_rows[None, :] < PREFILL) & (key_rows[None, :] <= row_ids[:, None])
    return jnp.where(is_prefill[:, None], before, key_rows[None, :] == row_ids[:, None])

def group_layer(inputs, out_full, gate_full, up_full, down_full, norm_gain):
    queries, fresh_kv, kv_pages, residual, page_table, shared_pages, cache_lens, prefill_offset = inputs
    key_pos, key_shared, key_owner = page_layout(jnp.arange(PAGES, dtype=jnp.int32), page_table, shared_pages)
    row_ids, is_prefill, decode_id, limit = row_layout(cache_lens, prefill_offset)
    visible = jnp.concatenate([cache_visible(key_pos, key_shared, key_owner, decode_id, limit), fresh_visible(row_ids, row_ids, is_prefill)], axis=1)
    cached = kv_pages.reshape(PAGES * PAGE, 2, KV_HEADS, HEAD)
    fresh = fresh_kv.reshape(ROWS, 2, KV_HEADS, HEAD)
    every_key = jnp.concatenate([cached, fresh], axis=0).astype(jnp.float32)
    grouped = HEADS // KV_HEADS
    query_heads = queries.astype(jnp.float32).reshape(ROWS, KV_HEADS, grouped, HEAD)
    score_scale = HEAD ** (-0.5)
    results = []
    for head_index in range(KV_HEADS):
        scores = jnp.einsum('rgh,kh->rgk', query_heads[:, head_index], every_key[:, 0, head_index]) * score_scale
        scores = jnp.where(visible[:, None, :], scores, NEG_FILL)
        row_peak = lax.optimization_barrier(jnp.max(scores, axis=2, keepdims=True))
        exponent = jnp.where(visible[:, None, :], jnp.exp(scores - row_peak), 0.0)
        row_total = lax.optimization_barrier(jnp.sum(exponent, axis=2, keepdims=True))
        rounded = lax.optimization_barrier(exponent.astype(jnp.bfloat16)).astype(jnp.float32)
        weighted = jnp.einsum('rgk,kh->rgh', rounded, every_key[:, 1, head_index])
        results.append(weighted / row_total)
    attended = jnp.stack(results, axis=1).reshape(ROWS, HEADS * HEAD).astype(jnp.bfloat16)
    feature_blocks = attended.astype(jnp.float32).reshape(ROWS, N_MLP, HEADS * HEAD // N_MLP)
    weight_blocks = out_full.reshape(N_MLP, HEADS * HEAD // N_MLP, D)
    partial_value = lax.optimization_barrier(jnp.einsum('rbf,bfd->brd', feature_blocks, weight_blocks).astype(jnp.bfloat16))
    projected = lax.optimization_barrier(jnp.sum(partial_value.astype(jnp.float32), axis=0))
    updated = residual.astype(jnp.float32) + projected
    normed = (updated * lax.rsqrt(lax.optimization_barrier(jnp.mean(updated * updated, axis=1, keepdims=True)) + EPSILON) * norm_gain).astype(jnp.bfloat16)
    normed_wide = normed.astype(jnp.float32)
    gate_act = jnp.dot(normed_wide, gate_full, preferred_element_type=jnp.float32)
    up_act = jnp.dot(normed_wide, up_full, preferred_element_type=jnp.float32)
    hidden = (jax.nn.silu(gate_act) * up_act).astype(jnp.bfloat16)
    hidden_blocks = hidden.astype(jnp.float32).reshape(ROWS, N_MLP, FF // N_MLP)
    down_blocks = down_full.reshape(N_MLP, FF // N_MLP, D)
    returned_parts = lax.optimization_barrier(jnp.einsum('rbf,bfd->brd', hidden_blocks, down_blocks).astype(jnp.bfloat16))
    returned = lax.optimization_barrier(jnp.sum(returned_parts.astype(jnp.float32), axis=0))
    return (updated + returned).astype(jnp.bfloat16)

def reference(queries, fresh_kv, kv_pages, residual, norm_gain, out_weight, gate_weight, up_weight, down_weight, page_table, shared_pages, cache_lens, prefill_offsets):
    out_full = out_weight.astype(jnp.float32)
    gate_full = gate_weight.astype(jnp.float32)
    up_full = up_weight.astype(jnp.float32)
    down_full = down_weight.astype(jnp.float32)

    def one_group(inputs):
        return group_layer(inputs, out_full, gate_full, up_full, down_full, norm_gain)
    return lax.map(one_group, (queries, fresh_kv, kv_pages, residual, page_table, shared_pages, cache_lens, prefill_offsets))
```

```python
import jax
import jax.numpy as jnp
from jax import lax
from jax.experimental import pallas as pl
from jax.experimental.pallas import tpu as pltpu
from jax.sharding import Mesh
from jax.sharding import PartitionSpec as P

HEAD = 128
PAGE = 128
SHARED_PAGES = 4
PRIVATE_PAGES = 12
DECODES = 16
PREFILL = 112
ROWS = 128
OWN_PAGES = 2
FRESH_PAD = 16
KEYS = OWN_PAGES * PAGE + FRESH_PAD
STATS = 16
NEG_FILL = -1e30
EPSILON = 1e-05
LONG = "y", "x", "z", "c"


def pieces(value):
    first = value.astype(jnp.bfloat16).astype(jnp.float32)
    rest = value - first
    second = rest.astype(jnp.bfloat16).astype(jnp.float32)
    return (first, second, rest - second)


def attention_kernel(
    place_ref, limit_ref, query_one, query_two, own_key, own_value, far_key, far_value, out_ref
):
    query = jnp.concatenate(
        [query_one[:, :HEAD], query_one[:, HEAD:], query_two[:, :HEAD], query_two[:, HEAD:]], axis=0
    )
    keys = jnp.concatenate([own_key[...], far_key[...]], axis=0)
    values = jnp.concatenate([own_value[...], far_value[...]], axis=0)
    scores = lax.dot_general(
        keys, query, (((1,), (1,)), ((), ())), preferred_element_type=jnp.float32
    ) * (HEAD ** (-0.5))
    token = lax.broadcasted_iota(jnp.int32, (PAGE, ROWS), 0)
    fresh = lax.broadcasted_iota(jnp.int32, (FRESH_PAD, ROWS), 0)
    row = lax.broadcasted_iota(jnp.int32, (FRESH_PAD, ROWS), 1)
    own_count = place_ref[3]
    seen = []
    for side in range(2):
        for page in range(OWN_PAGES):
            limit = limit_ref[pl.ds(side * OWN_PAGES + page, 1), :]
            seen.append((token < limit).astype(jnp.int32))
        key_row = place_ref[1 + side] + fresh
        before = jnp.where((key_row < PREFILL) & (key_row <= row), 1, 0)
        same = jnp.where(key_row == row, 1, 0)
        visible = jnp.where(row < PREFILL, before, same)
        seen.append(jnp.where(fresh < own_count, visible, 0))
    seen = jnp.concatenate(seen, axis=0)
    seen = jnp.concatenate([seen] * 4, axis=1) > 0
    scores = jnp.where(seen, scores, NEG_FILL)
    peak = jnp.max(scores, axis=0, keepdims=True)
    exps = jnp.where(seen, jnp.exp(scores - peak), 0.0)
    total = jnp.sum(exps, axis=0, keepdims=True)
    mixed = lax.dot_general(
        values,
        exps.astype(jnp.bfloat16),
        (((0,), (0,)), ((), ())),
        preferred_element_type=jnp.float32,
    )
    line = lax.broadcasted_iota(jnp.int32, (STATS, ROWS), 0)
    for half in range(2):
        stats = jnp.zeros((STATS, ROWS), jnp.float32)
        for head in range(2):
            column = (2 * half + head) * ROWS
            out_ref[half, pl.ds(head * HEAD, HEAD), :] = mixed[:, column : column + ROWS].astype(
                jnp.bfloat16
            )
            sent = pieces(peak[:, column : column + ROWS]) + pieces(
                total[:, column : column + ROWS]
            )
            for index, value in enumerate(sent):
                stats = jnp.where(line == 6 * head + index, value, stats)
        out_ref[half, pl.ds(2 * HEAD, STATS), :] = stats.astype(jnp.bfloat16)


def attention(place, limits, queries, own_kv, far_kv):
    kv_heads = own_kv.shape[1] // (2 * HEAD)
    chips = 2 * kv_heads

    def kv_spec(offset):
        return pl.BlockSpec((KEYS, HEAD), lambda j, place: (0, offset + j))

    return pl.pallas_call(
        attention_kernel,
        grid_spec=pltpu.PrefetchScalarGridSpec(
            num_scalar_prefetch=1,
            grid=(kv_heads,),
            in_specs=[
                pl.BlockSpec((2 * OWN_PAGES, ROWS), lambda j, place: (0, 0)),
                pl.BlockSpec((ROWS, 2 * HEAD), lambda j, place: (0, 4 * j + place[0])),
                pl.BlockSpec((ROWS, 2 * HEAD), lambda j, place: (0, 4 * j + 2 + place[0])),
                kv_spec(0),
                kv_spec(kv_heads),
                kv_spec(0),
                kv_spec(kv_heads),
            ],
            out_specs=pl.BlockSpec((2, 2 * HEAD + STATS, ROWS), lambda j, place: (j, 0, 0)),
        ),
        out_shape=jax.ShapeDtypeStruct((chips, 2 * HEAD + STATS, ROWS), jnp.bfloat16),
        compiler_params=pltpu.CompilerParams(vmem_limit_bytes=32 * 1024 * 1024),
        name="attention",
    )(place, limits, queries, queries, own_kv, own_kv, far_kv, far_kv)


def combine_kernel(parts_ref, out_ref):
    chips = parts_ref.shape[0]
    for head in range(2):
        peaks = []
        totals = []
        for source in range(chips):
            stats = parts_ref[source, pl.ds(2 * HEAD, STATS), :].astype(jnp.float32)
            base = 6 * head
            peaks.append(stats[base : base + 1] + stats[base + 1 : base + 2] + stats[base + 2 : base + 3])
            totals.append(
                stats[base + 3 : base + 4] + stats[base + 4 : base + 5] + stats[base + 5 : base + 6]
            )
        peak = peaks[0]
        for other in peaks[1:]:
            peak = jnp.maximum(peak, other)
        total = jnp.zeros_like(peak)
        mixed = jnp.zeros((HEAD, ROWS), jnp.float32)
        for source in range(chips):
            factor = jnp.exp(peaks[source] - peak)
            total = total + totals[source] * factor
            mixed = mixed + parts_ref[source, pl.ds(head * HEAD, HEAD), :].astype(jnp.float32) * factor
        attended = (mixed / total).astype(jnp.bfloat16)
        for copy in range(out_ref.shape[0]):
            out_ref[copy, pl.ds(head * HEAD, HEAD), :] = attended


def combine(parts, copies):
    return pl.pallas_call(
        combine_kernel,
        out_shape=jax.ShapeDtypeStruct((copies, 2 * HEAD, ROWS), jnp.bfloat16),
        compiler_params=pltpu.CompilerParams(vmem_limit_bytes=32 * 1024 * 1024),
        name="combine",
    )(parts)


def page_limits(page_ids, table, shared, lens, offset):
    shared_match = shared[None, :] == page_ids[:, None]
    is_shared = jnp.any(shared_match, axis=1)
    shared_slot = jnp.sum(
        jnp.where(shared_match, jnp.arange(SHARED_PAGES, dtype=jnp.int32)[None, :], 0), axis=1
    )
    own_match = table[None, :, :] == page_ids[:, None, None]
    decode = jnp.arange(DECODES, dtype=jnp.int32)[None, :, None] + 1
    owner = jnp.sum(jnp.where(own_match, decode, 0), axis=(1, 2)) - 1
    slot = jnp.arange(PRIVATE_PAGES, dtype=jnp.int32)[None, None, :]
    own_slot = jnp.sum(jnp.where(own_match, slot, 0), axis=(1, 2))
    base = jnp.where(is_shared, shared_slot, SHARED_PAGES + own_slot) * PAGE
    limit = jnp.concatenate([jnp.broadcast_to(offset, (PREFILL,)), lens])
    decode_id = jnp.arange(ROWS, dtype=jnp.int32) - PREFILL
    belongs = is_shared[:, None] | (
        (owner[:, None] == decode_id[None, :]) & (decode_id >= 0)[None, :]
    )
    return jnp.where(belongs, limit[None, :] - base[:, None], 0)


def swap(value):
    return lax.ppermute(value, "c", [(0, 1), (1, 0)])


def sum_to_rows(left, weights, core, contract):
    x_size, z_size = lax.axis_size("x"), lax.axis_size("z")
    half = weights.shape[0] // 2

    def product(which):
        piece = lax.dynamic_slice_in_dim(weights, which * half, half, 0)
        return lax.dot_general(
            left, piece, (((contract,), (1,)), ((), ())), preferred_element_type=jnp.float32
        ).reshape(x_size * ROWS, -1)

    far = swap(product(1 - core).astype(jnp.bfloat16))
    near = (product(core) + far.astype(jnp.float32)).astype(jnp.bfloat16)
    parts = lax.all_to_all(near, ("x", "z", "c"), 0, 0, tiled=True)
    rows = ROWS // (2 * z_size)
    parts = parts.reshape(x_size, z_size, 2, rows, half // HEAD, HEAD).astype(jnp.float32)
    summed = jnp.sum(parts, axis=1)
    return jnp.transpose(summed, (2, 1, 3, 0, 4)).reshape(rows, -1)


def local(
    queries,
    fresh_kv,
    kv_pages,
    residual,
    norm_gain,
    out_weight,
    gate_weight,
    up_weight,
    down_weight,
    page_table,
    shared_pages,
    cache_lens,
    prefill_offsets,
):
    y_size, x_size, z_size = lax.axis_size("y"), lax.axis_size("x"), lax.axis_size("z")
    core = lax.axis_index("c")
    mine = lax.axis_index("z") * 2 + core
    other = mine + 1 - 2 * core
    features = out_weight.shape[0]
    hidden_units = gate_weight.shape[1]
    own_rows = fresh_kv.shape[1]

    wide = lax.all_gather(
        jnp.concatenate([gate_weight, up_weight, out_weight.T, down_weight.T], axis=1),
        "y",
        axis=0,
        tiled=True,
    )
    joint = 2 * hidden_units

    own_kv = jnp.concatenate(
        [
            kv_pages.reshape(OWN_PAGES * PAGE, -1),
            fresh_kv[0],
            jnp.zeros((FRESH_PAD - own_rows, fresh_kv.shape[2]), jnp.bfloat16),
        ],
        axis=0,
    )
    far_kv = swap(own_kv)
    ids = jnp.arange(OWN_PAGES, dtype=jnp.int32)
    limits = page_limits(
        jnp.concatenate([mine * OWN_PAGES + ids, other * OWN_PAGES + ids]),
        page_table[0],
        shared_pages[0],
        cache_lens[0],
        prefill_offsets[0],
    )
    place = jnp.stack([core, mine * own_rows, other * own_rows, jnp.int32(own_rows)])
    parts = attention(place, limits, queries[0], own_kv, far_kv)
    parts = lax.all_to_all(parts, "z", 0, 0, tiled=True)
    attended = lax.all_to_all(combine(parts, x_size), "x", 0, 0, tiled=True)

    projected = sum_to_rows(attended, wide[:, joint : joint + features], core, 1)
    carried = lax.dynamic_slice_in_dim(residual[0], mine * own_rows, own_rows, 0)
    updated = carried.astype(jnp.float32) + projected
    normed = (
        updated
        * lax.rsqrt(jnp.mean(updated * updated, axis=1, keepdims=True) + EPSILON)
        * norm_gain
    ).astype(jnp.bfloat16)

    half = y_size // 2
    sent = jnp.transpose(normed.reshape(own_rows, 2, half, x_size, HEAD), (3, 1, 0, 2, 4))
    sent = jnp.broadcast_to(
        sent.reshape(x_size, 1, 2, own_rows, half * HEAD),
        (x_size, z_size, 2, own_rows, half * HEAD),
    ).reshape(x_size * ROWS, half * HEAD)
    near_rows = lax.all_to_all(sent, ("x", "z", "c"), 0, 0, tiled=True)
    far_rows = swap(near_rows)

    def partial(rows, which):
        piece = lax.dynamic_slice_in_dim(wide[:, :joint], which * half * HEAD, half * HEAD, 0)
        return jnp.dot(rows, piece, preferred_element_type=jnp.float32)

    gated = partial(near_rows, core) + partial(far_rows, 1 - core)
    gated = lax.all_to_all(gated.astype(jnp.bfloat16), "x", 0, 0, tiled=True)
    gated = jnp.sum(gated.reshape(x_size, ROWS, 2 * hidden_units).astype(jnp.float32), axis=0)
    gate_act, up_act = gated[:, :hidden_units], gated[:, hidden_units:]
    hidden = (jax.nn.silu(gate_act) * up_act).astype(jnp.bfloat16)
    hidden = jnp.broadcast_to(hidden[None], (x_size, ROWS, hidden_units))
    hidden = lax.all_to_all(hidden.reshape(x_size * ROWS, hidden_units), "x", 0, 0, tiled=True)

    returned = sum_to_rows(hidden, wide[:, joint + features :], core, 1)
    return (updated + returned).astype(jnp.bfloat16)[None]


def solution(mesh):
    cores = 2
    chips = mesh.shape["mlp"] // cores
    along = 4 if mesh.shape["grp"] % 16 == 0 else 2
    long_mesh = Mesh(
        mesh.devices.reshape(mesh.shape["grp"] // along, along, chips, cores), LONG
    )
    grp, mlp = ("y", "x"), ("z", "c")
    placed = (
        P(grp, None, None),
        P(grp, mlp, None),
        P(grp, mlp, None, None),
        P(grp, None, None),
        P(),
        P(mlp, grp),
        P(grp, mlp),
        P(grp, mlp),
        P(mlp, grp),
        P(grp, None, None),
        P(grp, None),
        P(grp, None),
        P(grp),
    )
    return jax.shard_map(
        local, mesh=long_mesh, in_specs=placed, out_specs=P(grp, mlp, None), check_vma=False
    )
```

```python
import functools

import jax
import jax.numpy as jnp
from jax import lax
from jax.experimental import pallas as pl
from jax.experimental.pallas import tpu as pltpu
from jax.sharding import Mesh
from jax.sharding import PartitionSpec as P

HEAD = 128
PAGE = 128
SHARED_PAGES = 4
PRIVATE_PAGES = 12
DECODES = 16
PREFILL = 112
ROWS = 128
OWN_PAGES = 2
FRESH_PAD = 16
KEYS = OWN_PAGES * PAGE + FRESH_PAD
STATS = 16
NEG_FILL = -1e30
EPSILON = 1e-05
LONG = "y", "x", "z", "c"
LIMIT = pltpu.CompilerParams(vmem_limit_bytes=32 * 1024 * 1024)
WIDE_LIMIT = pltpu.CompilerParams(vmem_limit_bytes=60 * 1024 * 1024)


def pieces(value):
    first = value.astype(jnp.bfloat16).astype(jnp.float32)
    rest = value - first
    second = rest.astype(jnp.bfloat16).astype(jnp.float32)
    return (first, second, rest - second)


def fill_limits(page_ids, lens_ref, offset_ref, table_ref, shared_ref, limit_ref):
    row = lax.broadcasted_iota(jnp.int32, (1, ROWS), 1)
    bound = jnp.full((1, ROWS), offset_ref[0], jnp.int32)
    for decode in range(DECODES):
        bound = jnp.where(row == PREFILL + decode, lens_ref[0, decode], bound)
    table, shared = table_ref[...], shared_ref[...]
    slot = lax.broadcasted_iota(jnp.int32, table.shape, 0)
    decode = lax.broadcasted_iota(jnp.int32, table.shape, 2) + 1
    shared_slot = lax.broadcasted_iota(jnp.int32, shared.shape, 1) + 1

    def whole(values):
        return jnp.sum(jnp.sum(values, axis=0), axis=1, keepdims=True)

    for index, page_id in enumerate(page_ids):
        listed = table == page_id
        owner = whole(jnp.where(listed, decode, 0)) - 1
        own_slot = whole(jnp.where(listed, slot, 0))
        prompt_slot = jnp.sum(
            jnp.where(shared == page_id, shared_slot, 0), axis=1, keepdims=True
        ) - 1
        prompt = jnp.broadcast_to(prompt_slot, row.shape) >= 0
        base = jnp.where(prompt_slot >= 0, prompt_slot, SHARED_PAGES + own_slot) * PAGE
        mine = (row >= PREFILL) & (row - PREFILL == owner)
        limit_ref[index : index + 1, :] = jnp.where(prompt | mine, bound - base, 0)


def attention_kernel(
    own_rows,
    core_ref,
    lens_ref,
    offset_ref,
    table_ref,
    shared_ref,
    query_one,
    query_two,
    own_key,
    own_value,
    far_key,
    far_value,
    out_ref,
    limit_ref,
):
    core = lax.axis_index("c")
    mine = 2 * lax.axis_index("z") + core
    sides = (mine, mine + 1 - 2 * core)

    @pl.when(pl.program_id(0) == 0)
    def _():
        page_ids = [side * OWN_PAGES + page for side in sides for page in range(OWN_PAGES)]
        fill_limits(page_ids, lens_ref, offset_ref, table_ref, shared_ref, limit_ref)

    query = jnp.concatenate(
        [query_one[:, :HEAD], query_one[:, HEAD:], query_two[:, :HEAD], query_two[:, HEAD:]], axis=0
    )
    keys = jnp.concatenate([own_key[...], far_key[...]], axis=0)
    values = jnp.concatenate([own_value[...], far_value[...]], axis=0)
    scores = lax.dot_general(
        keys, query, (((1,), (1,)), ((), ())), preferred_element_type=jnp.float32
    ) * (HEAD ** (-0.5))
    token = lax.broadcasted_iota(jnp.int32, (PAGE, ROWS), 0)
    fresh = lax.broadcasted_iota(jnp.int32, (FRESH_PAD, ROWS), 0)
    row = lax.broadcasted_iota(jnp.int32, (FRESH_PAD, ROWS), 1)
    seen = []
    for side in range(2):
        for page in range(OWN_PAGES):
            limit = limit_ref[pl.ds(side * OWN_PAGES + page, 1), :]
            seen.append((token < limit).astype(jnp.int32))
        key_row = sides[side] * own_rows + fresh
        before = jnp.where((key_row < PREFILL) & (key_row <= row), 1, 0)
        same = jnp.where(key_row == row, 1, 0)
        visible = jnp.where(row < PREFILL, before, same)
        seen.append(jnp.where(fresh < own_rows, visible, 0))
    seen = jnp.concatenate(seen, axis=0)
    seen = jnp.concatenate([seen] * 4, axis=1) > 0
    scores = jnp.where(seen, scores, NEG_FILL)
    peak = jnp.max(scores, axis=0, keepdims=True)
    exps = jnp.where(seen, jnp.exp(scores - peak), 0.0)
    total = jnp.sum(exps, axis=0, keepdims=True)
    mixed = lax.dot_general(
        values,
        exps.astype(jnp.bfloat16),
        (((0,), (0,)), ((), ())),
        preferred_element_type=jnp.float32,
    )
    line = lax.broadcasted_iota(jnp.int32, (STATS, ROWS), 0)
    for half in range(2):
        stats = jnp.zeros((STATS, ROWS), jnp.float32)
        for head in range(2):
            column = (2 * half + head) * ROWS
            out_ref[half, pl.ds(head * HEAD, HEAD), :] = mixed[:, column : column + ROWS].astype(
                jnp.bfloat16
            )
            sent = pieces(peak[:, column : column + ROWS]) + pieces(
                total[:, column : column + ROWS]
            )
            for index, value in enumerate(sent):
                stats = jnp.where(line == 6 * head + index, value, stats)
        out_ref[half, pl.ds(2 * HEAD, STATS), :] = stats.astype(jnp.bfloat16)


def attention(core, own_rows, lens, offset, table, shared, queries, own_kv, far_kv):
    kv_heads = own_kv.shape[1] // (2 * HEAD)
    chips = 2 * kv_heads
    smem = pl.BlockSpec(memory_space=pltpu.SMEM)

    def kv_spec(offset):
        return pl.BlockSpec((KEYS, HEAD), lambda j, core: (0, offset + j))

    return pl.pallas_call(
        functools.partial(attention_kernel, own_rows),
        grid_spec=pltpu.PrefetchScalarGridSpec(
            num_scalar_prefetch=1,
            grid=(kv_heads,),
            in_specs=[
                smem,
                smem,
                pl.BlockSpec(table.shape, lambda j, core: (0, 0, 0)),
                pl.BlockSpec(shared.shape, lambda j, core: (0, 0)),
                pl.BlockSpec((ROWS, 2 * HEAD), lambda j, core: (0, 4 * j + core[0])),
                pl.BlockSpec((ROWS, 2 * HEAD), lambda j, core: (0, 4 * j + 2 + core[0])),
                kv_spec(0),
                kv_spec(kv_heads),
                kv_spec(0),
                kv_spec(kv_heads),
            ],
            out_specs=pl.BlockSpec((2, 2 * HEAD + STATS, ROWS), lambda j, core: (j, 0, 0)),
            scratch_shapes=[pltpu.VMEM((2 * OWN_PAGES, ROWS), jnp.int32)],
        ),
        out_shape=jax.ShapeDtypeStruct((chips, 2 * HEAD + STATS, ROWS), jnp.bfloat16),
        compiler_params=LIMIT,
        name="attention",
    )(core, lens, offset, table, shared, queries, queries, own_kv, own_kv, far_kv, far_kv)


def combine_kernel(parts_ref, out_ref):
    chips = parts_ref.shape[0]
    for head in range(2):
        peaks = []
        totals = []
        for source in range(chips):
            stats = parts_ref[source, pl.ds(2 * HEAD, STATS), :].astype(jnp.float32)
            lines = [stats[6 * head + k : 6 * head + k + 1] for k in range(6)]
            peaks.append(lines[0] + lines[1] + lines[2])
            totals.append(lines[3] + lines[4] + lines[5])
        peak = peaks[0]
        for other in peaks[1:]:
            peak = jnp.maximum(peak, other)
        total = jnp.zeros_like(peak)
        mixed = jnp.zeros((HEAD, ROWS), jnp.float32)
        for source in range(chips):
            factor = jnp.exp(peaks[source] - peak)
            total = total + totals[source] * factor
            mixed = mixed + parts_ref[source, pl.ds(head * HEAD, HEAD), :].astype(jnp.float32) * factor
        attended = (mixed / total).T.astype(jnp.bfloat16)
        for copy in range(out_ref.shape[0]):
            out_ref[copy, :, head * HEAD : (head + 1) * HEAD] = attended


def combine(parts, copies):
    return pl.pallas_call(
        combine_kernel,
        out_shape=jax.ShapeDtypeStruct((copies, ROWS, 2 * HEAD), jnp.bfloat16),
        compiler_params=LIMIT,
        name="combine",
    )(parts)


def pack_kernel(
    out_ref, gate_ref, up_ref, down_ref, pages_ref, fresh_ref, weights_ref, kv_ref, spread_ref
):
    units = gate_ref.shape[1]
    weights_ref[:, :HEAD] = out_ref[:HEAD, :]
    weights_ref[:, HEAD : 2 * HEAD] = out_ref[HEAD:, :]
    weights_ref[:, 2 * HEAD : 2 * HEAD + units] = gate_ref[...]
    weights_ref[:, 2 * HEAD + units :] = up_ref[...]
    for page in range(OWN_PAGES):
        kv_ref[page * PAGE : (page + 1) * PAGE, :] = pages_ref[page]
    rest = FRESH_PAD - fresh_ref.shape[0]
    fresh = fresh_ref[...]
    if rest:
        fresh = jnp.concatenate([fresh, jnp.zeros((rest, fresh.shape[1]), jnp.bfloat16)], axis=0)
    kv_ref[OWN_PAGES * PAGE :, :] = fresh
    for copy in range(spread_ref.shape[0]):
        spread_ref[copy] = down_ref[...]


def pack(out_weight, gate_weight, up_weight, down_weight, pages, fresh, copies):
    width = 2 * HEAD + 2 * gate_weight.shape[1]
    return pl.pallas_call(
        pack_kernel,
        out_shape=(
            jax.ShapeDtypeStruct((HEAD, width), jnp.bfloat16),
            jax.ShapeDtypeStruct((KEYS, fresh.shape[1]), jnp.bfloat16),
            jax.ShapeDtypeStruct((copies,) + down_weight.shape, jnp.bfloat16),
        ),
        compiler_params=WIDE_LIMIT,
        name="pack",
    )(out_weight, gate_weight, up_weight, down_weight, pages, fresh)


def out_kernel(place_ref, attended_ref, weights_ref, *rest):
    result_ref = rest[-1]
    weights = jnp.concatenate([weights_ref[:, :HEAD], weights_ref[:, HEAD:]], axis=0)
    product = jnp.dot(attended_ref[...], weights, preferred_element_type=jnp.float32)
    if len(rest) == 2:
        product = product + rest[0][...].astype(jnp.float32)
    result_ref[...] = product.astype(jnp.bfloat16)


def out_product(half, attended, weights, far=None):
    rows = attended.shape[0]
    steps = weights.shape[0] // (2 * HEAD)
    column = pl.BlockSpec((rows, HEAD), lambda i, half: (0, i))
    return pl.pallas_call(
        out_kernel,
        grid_spec=pltpu.PrefetchScalarGridSpec(
            num_scalar_prefetch=1,
            grid=(steps,),
            in_specs=[
                pl.BlockSpec((rows, 2 * HEAD), lambda i, half: (0, 0)),
                pl.BlockSpec((HEAD, 2 * HEAD), lambda i, half: (half[0] * steps + i, 0)),
            ]
            + ([] if far is None else [column]),
            out_specs=column,
        ),
        out_shape=jax.ShapeDtypeStruct((rows, steps * HEAD), jnp.bfloat16),
        compiler_params=LIMIT,
        name="out_product",
    )(half, attended, weights, *(() if far is None else (far,)))


def norm_kernel(place_ref, parts_ref, residual_ref, gain_ref, updated_ref, sent_ref):
    x_size, z_size = parts_ref.shape[:2]
    blocks = parts_ref.shape[4] // HEAD
    square = jnp.zeros((parts_ref.shape[3], 1), jnp.float32)
    for x in range(x_size):
        for core in range(2):
            summed = parts_ref[x, 0, core].astype(jnp.float32)
            for z in range(1, z_size):
                summed = summed + parts_ref[x, z, core].astype(jnp.float32)
            for block in range(blocks):
                column = ((core * blocks + block) * x_size + x) * HEAD
                value = summed[:, block * HEAD : (block + 1) * HEAD]
                value = value + residual_ref[0, :, column : column + HEAD].astype(jnp.float32)
                square = square + jnp.sum(value * value, axis=1, keepdims=True)
                updated_ref[:, column : column + HEAD] = value
    scale = lax.rsqrt(square / (2 * x_size * blocks * HEAD) + EPSILON)
    for x in range(x_size):
        for core in range(2):
            normed = []
            for block in range(blocks):
                column = ((core * blocks + block) * x_size + x) * HEAD
                value = updated_ref[:, column : column + HEAD] * scale
                normed.append(value * gain_ref[:, column : column + HEAD])
            normed = jnp.concatenate(normed, axis=1).astype(jnp.bfloat16)
            for z in range(z_size):
                sent_ref[x, z, core] = normed


def add_and_norm(place, parts, residual, gain):
    rows, width = parts.shape[3], residual.shape[2]
    return pl.pallas_call(
        norm_kernel,
        grid_spec=pltpu.PrefetchScalarGridSpec(
            num_scalar_prefetch=1,
            grid=(1,),
            in_specs=[
                pl.BlockSpec(parts.shape, lambda i, place: (0,) * 5),
                pl.BlockSpec((1, rows, width), lambda i, place: (0, place[0], 0)),
                pl.BlockSpec((1, width), lambda i, place: (0, 0)),
            ],
            out_specs=[
                pl.BlockSpec((rows, width), lambda i, place: (0, 0)),
                pl.BlockSpec(parts.shape, lambda i, place: (0,) * 5),
            ],
        ),
        out_shape=(
            jax.ShapeDtypeStruct((rows, width), jnp.float32),
            jax.ShapeDtypeStruct(parts.shape, jnp.bfloat16),
        ),
        compiler_params=LIMIT,
        name="add_and_norm",
    )(place, parts, residual, gain.reshape(1, -1))


def times_down(hidden, down_ref):
    return jnp.concatenate(
        [
            jnp.dot(hidden, down_ref[block], preferred_element_type=jnp.float32)
            for block in range(down_ref.shape[0])
        ],
        axis=1,
    )


def hidden_kernel(half_ref, parts_ref, down_ref, hidden_ref, far_ref):
    @pl.when(pl.program_id(0) == 0)
    def _():
        summed = parts_ref[0].astype(jnp.float32)
        for source in range(1, parts_ref.shape[0]):
            summed = summed + parts_ref[source].astype(jnp.float32)
        units = summed.shape[1] // 2
        gate = summed[:, :units]
        hidden_ref[...] = (gate / (1.0 + jnp.exp(-gate)) * summed[:, units:]).astype(jnp.bfloat16)

    far_ref[...] = times_down(hidden_ref[...], down_ref).astype(jnp.bfloat16)


def down_spec(down, steps):
    blocks = down.shape[0] // (2 * steps)
    return pl.BlockSpec((blocks,) + down.shape[1:], lambda i, half: (half[0] * steps + i, 0, 0))


def hidden_product(half, parts, down):
    units = down.shape[1]
    steps = 4 if down.shape[0] % 8 == 0 else 1
    width = down.shape[0] // 2 * HEAD
    return pl.pallas_call(
        hidden_kernel,
        grid_spec=pltpu.PrefetchScalarGridSpec(
            num_scalar_prefetch=1,
            grid=(steps,),
            in_specs=[
                pl.BlockSpec(parts.shape, lambda i, half: (0, 0, 0)),
                down_spec(down, steps),
            ],
            out_specs=[
                pl.BlockSpec((ROWS, units), lambda i, half: (0, 0)),
                pl.BlockSpec((ROWS, width // steps), lambda i, half: (0, i)),
            ],
        ),
        out_shape=(
            jax.ShapeDtypeStruct((ROWS, units), jnp.bfloat16),
            jax.ShapeDtypeStruct((ROWS, width), jnp.bfloat16),
        ),
        compiler_params=LIMIT,
        name="hidden_product",
    )(half, parts, down)


def down_kernel(half_ref, hidden_ref, down_ref, far_ref, near_ref):
    product = times_down(hidden_ref[...], down_ref) + far_ref[...].astype(jnp.float32)
    near_ref[...] = product.astype(jnp.bfloat16)


def down_product(half, hidden, down, far):
    steps = 4 if down.shape[0] % 8 == 0 else 1
    column = pl.BlockSpec((ROWS, far.shape[1] // steps), lambda i, half: (0, i))
    return pl.pallas_call(
        down_kernel,
        grid_spec=pltpu.PrefetchScalarGridSpec(
            num_scalar_prefetch=1,
            grid=(steps,),
            in_specs=[
                pl.BlockSpec(hidden.shape, lambda i, half: (0, 0)),
                down_spec(down, steps),
                column,
            ],
            out_specs=column,
        ),
        out_shape=jax.ShapeDtypeStruct(far.shape, jnp.bfloat16),
        compiler_params=LIMIT,
        name="down_product",
    )(half, hidden, down, far)


def swap(value):
    return lax.ppermute(value, "c", [(0, 1), (1, 0)])


def local(
    queries,
    fresh_kv,
    kv_pages,
    residual,
    norm_gain,
    out_weight,
    gate_weight,
    up_weight,
    down_weight,
    page_table,
    shared_pages,
    cache_lens,
    prefill_offsets,
):
    y_size, x_size, z_size = lax.axis_size("y"), lax.axis_size("x"), lax.axis_size("z")
    core = lax.axis_index("c")
    mine = lax.axis_index("z") * 2 + core
    near_half, far_half = core.reshape(1), (1 - core).reshape(1)
    own_rows = fresh_kv.shape[1]
    half = y_size // 2

    packed, own_kv, spread = pack(
        out_weight, gate_weight, up_weight, down_weight, kv_pages[0], fresh_kv[0], x_size
    )
    weights = lax.all_gather(packed, "y", axis=0, tiled=True)
    far_kv = swap(own_kv)
    down = lax.all_to_all(spread, "x", 0, 0, tiled=True)
    parts = attention(
        near_half,
        own_rows,
        cache_lens,
        prefill_offsets,
        jnp.transpose(page_table, (2, 0, 1)),
        shared_pages,
        queries[0],
        own_kv,
        far_kv,
    )
    parts, down = lax.optimization_barrier((parts, down))
    down = lax.all_gather(down, "y", axis=0, tiled=True)
    parts = lax.all_to_all(parts, "z", 0, 0, tiled=True)
    attended = lax.all_to_all(combine(parts, x_size), "x", 0, 0, tiled=True)
    attended = attended.reshape(x_size * ROWS, 2 * HEAD)

    far = swap(out_product(far_half, attended, weights))
    parts = out_product(near_half, attended, weights, far)
    parts = lax.all_to_all(parts, ("x", "z", "c"), 0, 0, tiled=True)
    parts = parts.reshape(x_size, z_size, 2, own_rows, half * HEAD)
    updated, sent = add_and_norm(mine.reshape(1), parts, residual, norm_gain)
    near_rows = lax.all_to_all(
        sent.reshape(x_size * ROWS, half * HEAD), ("x", "z", "c"), 0, 0, tiled=True
    )
    far_rows = swap(near_rows)

    def partial(rows, which):
        piece = lax.dynamic_slice_in_dim(weights, which * half * HEAD, half * HEAD, 0)
        return jnp.dot(rows, piece[:, 2 * HEAD :], preferred_element_type=jnp.float32)

    gated = partial(near_rows, core) + partial(far_rows, 1 - core)
    gated = lax.all_to_all(gated.astype(jnp.bfloat16), "x", 0, 0, tiled=True)
    gated = gated.reshape(x_size, ROWS, gated.shape[1])
    hidden, far = hidden_product(far_half, gated, down)
    parts = down_product(near_half, hidden, down, swap(far))
    parts = lax.all_to_all(parts, ("z", "c"), 0, 0, tiled=True)
    parts = parts.reshape(z_size, 2, own_rows, parts.shape[1])
    returned = jnp.transpose(jnp.sum(parts.astype(jnp.float32), axis=0), (1, 0, 2))
    return (updated + returned.reshape(own_rows, -1)).astype(jnp.bfloat16)[None]


def solution(mesh):
    cores = 2
    chips = mesh.shape["mlp"] // cores
    along = 4 if mesh.shape["grp"] % 16 == 0 else 2
    long_mesh = Mesh(
        mesh.devices.reshape(mesh.shape["grp"] // along, along, chips, cores), LONG
    )
    grp, mlp = ("y", "x"), ("z", "c")
    placed = (
        P(grp, None, None),
        P(grp, mlp, None),
        P(grp, mlp, None, None),
        P(grp, None, None),
        P(),
        P(mlp, grp),
        P(grp, mlp),
        P(grp, mlp),
        P(mlp, grp),
        P(grp, None, None),
        P(grp, None),
        P(grp, None),
        P(grp),
    )
    return jax.shard_map(
        local, mesh=long_mesh, in_specs=placed, out_specs=P(grp, mlp, None), check_vma=False
    )
```

```python
import functools

import jax
import jax.numpy as jnp
from jax import lax
from jax.experimental import pallas as pl
from jax.experimental.pallas import tpu as pltpu
from jax.sharding import Mesh
from jax.sharding import PartitionSpec as P

HEAD = 128
PAGE = 128
SHARED_PAGES = 4
PRIVATE_PAGES = 12
DECODES = 16
PREFILL = 112
ROWS = 128
OWN_PAGES = 2
FRESH_PAD = 16
KEYS = OWN_PAGES * PAGE + FRESH_PAD
STATS = 16
NEG_FILL = -1e30
EPSILON = 1e-05
LONG = "y", "x", "z", "c"
LIMIT = pltpu.CompilerParams(vmem_limit_bytes=32 * 1024 * 1024)
WIDE_LIMIT = pltpu.CompilerParams(vmem_limit_bytes=60 * 1024 * 1024)


def pieces(value):
    first = value.astype(jnp.bfloat16).astype(jnp.float32)
    rest = value - first
    second = rest.astype(jnp.bfloat16).astype(jnp.float32)
    return (first, second, rest - second)


def fill_limits(page_ids, lens_ref, offset_ref, table_ref, shared_ref, limit_ref):
    row = lax.broadcasted_iota(jnp.int32, (1, ROWS), 1)
    bound = jnp.full((1, ROWS), offset_ref[0], jnp.int32)
    for decode in range(DECODES):
        bound = jnp.where(row == PREFILL + decode, lens_ref[0, decode], bound)
    table, shared = table_ref[...], shared_ref[...]
    slot = lax.broadcasted_iota(jnp.int32, table.shape, 0)
    decode = lax.broadcasted_iota(jnp.int32, table.shape, 2) + 1
    shared_slot = lax.broadcasted_iota(jnp.int32, shared.shape, 1) + 1

    def whole(values):
        return jnp.sum(jnp.sum(values, axis=0), axis=1, keepdims=True)

    for index, page_id in enumerate(page_ids):
        listed = table == page_id
        owner = whole(jnp.where(listed, decode, 0)) - 1
        own_slot = whole(jnp.where(listed, slot, 0))
        prompt_slot = jnp.sum(
            jnp.where(shared == page_id, shared_slot, 0), axis=1, keepdims=True
        ) - 1
        prompt = jnp.broadcast_to(prompt_slot, row.shape) >= 0
        base = jnp.where(prompt_slot >= 0, prompt_slot, SHARED_PAGES + own_slot) * PAGE
        mine = (row >= PREFILL) & (row - PREFILL == owner)
        limit_ref[index : index + 1, :] = jnp.where(prompt | mine, bound - base, 0)


def attention_kernel(
    own_rows,
    core_ref,
    mine_ref,
    limit_ref,
    residual_ref,
    query_one,
    query_two,
    own_key,
    own_value,
    far_key,
    far_value,
    out_ref,
    carried_ref,
):
    @pl.when(pl.program_id(0) == 0)
    def _():
        carried_ref[...] = residual_ref[0].astype(jnp.float32)

    core = lax.axis_index("c")
    mine = 2 * lax.axis_index("z") + core
    sides = (mine, mine + 1 - 2 * core)
    query = jnp.concatenate(
        [query_one[:, :HEAD], query_one[:, HEAD:], query_two[:, :HEAD], query_two[:, HEAD:]], axis=0
    )
    keys = jnp.concatenate([own_key[...], far_key[...]], axis=0)
    values = jnp.concatenate([own_value[...], far_value[...]], axis=0)
    scores = lax.dot_general(
        keys, query, (((1,), (1,)), ((), ())), preferred_element_type=jnp.float32
    ) * (HEAD ** (-0.5))
    token = lax.broadcasted_iota(jnp.int32, (PAGE, ROWS), 0)
    fresh = lax.broadcasted_iota(jnp.int32, (FRESH_PAD, ROWS), 0)
    row = lax.broadcasted_iota(jnp.int32, (FRESH_PAD, ROWS), 1)
    seen = []
    for side in range(2):
        for page in range(OWN_PAGES):
            limit = limit_ref[pl.ds(side * OWN_PAGES + page, 1), :]
            seen.append((token < limit).astype(jnp.int32))
        key_row = sides[side] * own_rows + fresh
        before = jnp.where((key_row < PREFILL) & (key_row <= row), 1, 0)
        same = jnp.where(key_row == row, 1, 0)
        visible = jnp.where(row < PREFILL, before, same)
        seen.append(jnp.where(fresh < own_rows, visible, 0))
    seen = jnp.concatenate(seen, axis=0)
    seen = jnp.concatenate([seen] * 4, axis=1) > 0
    scores = jnp.where(seen, scores, NEG_FILL)
    peak = jnp.max(scores, axis=0, keepdims=True)
    exps = jnp.where(seen, jnp.exp(scores - peak), 0.0)
    total = jnp.sum(exps, axis=0, keepdims=True)
    mixed = lax.dot_general(
        values,
        exps.astype(jnp.bfloat16),
        (((0,), (0,)), ((), ())),
        preferred_element_type=jnp.float32,
    )
    line = lax.broadcasted_iota(jnp.int32, (STATS, ROWS), 0)
    for half in range(2):
        stats = jnp.zeros((STATS, ROWS), jnp.float32)
        for head in range(2):
            column = (2 * half + head) * ROWS
            out_ref[half, pl.ds(head * HEAD, HEAD), :] = mixed[:, column : column + ROWS].astype(
                jnp.bfloat16
            )
            sent = pieces(peak[:, column : column + ROWS]) + pieces(
                total[:, column : column + ROWS]
            )
            for index, value in enumerate(sent):
                stats = jnp.where(line == 6 * head + index, value, stats)
        out_ref[half, pl.ds(2 * HEAD, STATS), :] = stats.astype(jnp.bfloat16)


def attention(core, mine, own_rows, limits, residual, queries, own_kv, far_kv):
    kv_heads = own_kv.shape[1] // (2 * HEAD)
    chips = 2 * kv_heads
    width = residual.shape[2]

    def kv_spec(offset):
        return pl.BlockSpec((KEYS, HEAD), lambda j, core, mine: (0, offset + j))

    return pl.pallas_call(
        functools.partial(attention_kernel, own_rows),
        grid_spec=pltpu.PrefetchScalarGridSpec(
            num_scalar_prefetch=2,
            grid=(kv_heads,),
            in_specs=[
                pl.BlockSpec(limits.shape, lambda j, core, mine: (0, 0)),
                pl.BlockSpec((1, own_rows, width), lambda j, core, mine: (0, mine[0], 0)),
                pl.BlockSpec((ROWS, 2 * HEAD), lambda j, core, mine: (0, 4 * j + core[0])),
                pl.BlockSpec((ROWS, 2 * HEAD), lambda j, core, mine: (0, 4 * j + 2 + core[0])),
                kv_spec(0),
                kv_spec(kv_heads),
                kv_spec(0),
                kv_spec(kv_heads),
            ],
            out_specs=[
                pl.BlockSpec((2, 2 * HEAD + STATS, ROWS), lambda j, core, mine: (j, 0, 0)),
                pl.BlockSpec((own_rows, width), lambda j, core, mine: (0, 0)),
            ],
        ),
        out_shape=(
            jax.ShapeDtypeStruct((chips, 2 * HEAD + STATS, ROWS), jnp.bfloat16),
            jax.ShapeDtypeStruct((own_rows, width), jnp.float32),
        ),
        compiler_params=WIDE_LIMIT,
        name="attention",
    )(core, mine, limits, residual, queries, queries, own_kv, own_kv, far_kv, far_kv)


def combine_kernel(parts_ref, out_ref):
    chips = parts_ref.shape[0]
    for head in range(2):
        peaks = []
        totals = []
        for source in range(chips):
            stats = parts_ref[source, pl.ds(2 * HEAD, STATS), :].astype(jnp.float32)
            lines = [stats[6 * head + k : 6 * head + k + 1] for k in range(6)]
            peaks.append(lines[0] + lines[1] + lines[2])
            totals.append(lines[3] + lines[4] + lines[5])
        peak = peaks[0]
        for other in peaks[1:]:
            peak = jnp.maximum(peak, other)
        total = jnp.zeros_like(peak)
        mixed = jnp.zeros((HEAD, ROWS), jnp.float32)
        for source in range(chips):
            factor = jnp.exp(peaks[source] - peak)
            total = total + totals[source] * factor
            mixed = mixed + parts_ref[source, pl.ds(head * HEAD, HEAD), :].astype(jnp.float32) * factor
        attended = (mixed / total).T.astype(jnp.bfloat16)
        for copy in range(out_ref.shape[0]):
            out_ref[copy, :, head * HEAD : (head + 1) * HEAD] = attended


def combine(parts, copies):
    return pl.pallas_call(
        combine_kernel,
        out_shape=jax.ShapeDtypeStruct((copies, ROWS, 2 * HEAD), jnp.bfloat16),
        compiler_params=LIMIT,
        name="combine",
    )(parts)


def pack_kernel(
    lens_ref,
    offset_ref,
    table_ref,
    shared_ref,
    out_ref,
    gate_ref,
    up_ref,
    down_ref,
    pages_ref,
    fresh_ref,
    weights_ref,
    kv_ref,
    spread_ref,
    limit_ref,
):
    column = 0
    for source in (out_ref, gate_ref, up_ref):
        for row in range(0, source.shape[0], HEAD):
            width = source.shape[1]
            weights_ref[:, column : column + width] = source[row : row + HEAD, :]
            column += width
    for copy in range(spread_ref.shape[0]):
        spread_ref[copy] = down_ref[...]
    for page in range(OWN_PAGES):
        kv_ref[page * PAGE : (page + 1) * PAGE, :] = pages_ref[page]
    own_rows = fresh_ref.shape[0]
    rest = FRESH_PAD - own_rows
    fresh = fresh_ref[...]
    if rest:
        fresh = jnp.concatenate([fresh, jnp.zeros((rest, fresh.shape[1]), jnp.bfloat16)], axis=0)
    kv_ref[OWN_PAGES * PAGE :, :] = fresh
    core = lax.axis_index("c")
    mine = 2 * lax.axis_index("z") + core
    sides = (mine, mine + 1 - 2 * core)
    page_ids = [side * OWN_PAGES + page for side in sides for page in range(OWN_PAGES)]
    fill_limits(page_ids, lens_ref, offset_ref, table_ref, shared_ref, limit_ref)


def pack(copies, lens, offset, table, shared, weights, down_weight, pages, fresh):
    width = sum((piece.shape[0] // HEAD) * piece.shape[1] for piece in weights)
    smem = pl.BlockSpec(memory_space=pltpu.SMEM)
    vmem = pl.BlockSpec(memory_space=pltpu.VMEM)
    return pl.pallas_call(
        pack_kernel,
        in_specs=[smem] * 2 + [vmem] * 8,
        out_shape=(
            jax.ShapeDtypeStruct((HEAD, width), jnp.bfloat16),
            jax.ShapeDtypeStruct((KEYS, fresh.shape[1]), jnp.bfloat16),
            jax.ShapeDtypeStruct((copies,) + down_weight.shape, jnp.bfloat16),
            jax.ShapeDtypeStruct((2 * OWN_PAGES, ROWS), jnp.int32),
        ),
        compiler_params=WIDE_LIMIT,
        name="pack",
    )(lens, offset, table, shared, *weights, down_weight, pages, fresh)


def out_kernel(place_ref, attended_ref, weights_ref, *rest):
    result_ref = rest[-1]
    weights = jnp.concatenate([weights_ref[:, :HEAD], weights_ref[:, HEAD:]], axis=0)
    product = jnp.dot(attended_ref[...], weights, preferred_element_type=jnp.float32)
    if len(rest) == 2:
        product = product + rest[0][...].astype(jnp.float32)
    result_ref[...] = product.astype(jnp.bfloat16)


def out_product(half, attended, weights, far=None):
    rows = attended.shape[0]
    steps = weights.shape[0] // (2 * HEAD)
    column = pl.BlockSpec((rows, HEAD), lambda i, half: (0, i))
    return pl.pallas_call(
        out_kernel,
        grid_spec=pltpu.PrefetchScalarGridSpec(
            num_scalar_prefetch=1,
            grid=(steps,),
            in_specs=[
                pl.BlockSpec((rows, 2 * HEAD), lambda i, half: (0, 0)),
                pl.BlockSpec((HEAD, 2 * HEAD), lambda i, half: (half[0] * steps + i, 0)),
            ]
            + ([] if far is None else [column]),
            out_specs=column,
        ),
        out_shape=jax.ShapeDtypeStruct((rows, steps * HEAD), jnp.bfloat16),
        compiler_params=LIMIT,
        name="out_product",
    )(half, attended, weights, *(() if far is None else (far,)))


def norm_kernel(parts_ref, residual_ref, gain_ref, updated_ref, sent_ref):
    x_size, z_size = parts_ref.shape[:2]
    blocks = parts_ref.shape[4] // HEAD
    square = jnp.zeros((parts_ref.shape[3], 1), jnp.float32)
    for x in range(x_size):
        for core in range(2):
            summed = parts_ref[x, 0, core].astype(jnp.float32)
            for z in range(1, z_size):
                summed = summed + parts_ref[x, z, core].astype(jnp.float32)
            for block in range(blocks):
                column = ((core * blocks + block) * x_size + x) * HEAD
                value = summed[:, block * HEAD : (block + 1) * HEAD]
                value = value + residual_ref[:, column : column + HEAD]
                square = square + jnp.sum(value * value, axis=1, keepdims=True)
                updated_ref[:, column : column + HEAD] = value
    scale = lax.rsqrt(square / (2 * x_size * blocks * HEAD) + EPSILON)
    for x in range(x_size):
        for core in range(2):
            normed = []
            for block in range(blocks):
                column = ((core * blocks + block) * x_size + x) * HEAD
                value = updated_ref[:, column : column + HEAD] * scale
                normed.append(value * gain_ref[:, column : column + HEAD])
            normed = jnp.concatenate(normed, axis=1).astype(jnp.bfloat16)
            for z in range(z_size):
                sent_ref[x, z, core] = normed


def add_and_norm(parts, residual, gain):
    return pl.pallas_call(
        norm_kernel,
        out_shape=(
            jax.ShapeDtypeStruct(residual.shape, jnp.float32),
            jax.ShapeDtypeStruct(parts.shape, jnp.bfloat16),
        ),
        compiler_params=LIMIT,
        name="add_and_norm",
    )(parts, residual, gain.reshape(1, -1))


def times_down(hidden, down_ref):
    return jnp.concatenate(
        [
            jnp.dot(hidden, down_ref[block], preferred_element_type=jnp.float32)
            for block in range(down_ref.shape[0])
        ],
        axis=1,
    )


def hidden_kernel(half_ref, parts_ref, down_ref, hidden_ref, far_ref):
    @pl.when(pl.program_id(0) == 0)
    def _():
        summed = parts_ref[0].astype(jnp.float32)
        for source in range(1, parts_ref.shape[0]):
            summed = summed + parts_ref[source].astype(jnp.float32)
        units = summed.shape[1] // 2
        gate = summed[:, :units]
        hidden_ref[...] = (gate / (1.0 + jnp.exp(-gate)) * summed[:, units:]).astype(jnp.bfloat16)

    far_ref[...] = times_down(hidden_ref[...], down_ref).astype(jnp.bfloat16)


def down_spec(down, steps):
    blocks = down.shape[0] // (2 * steps)
    return pl.BlockSpec((blocks,) + down.shape[1:], lambda i, half: (half[0] * steps + i, 0, 0))


def hidden_product(half, parts, down):
    units = down.shape[1]
    steps = 4 if down.shape[0] % 8 == 0 else 1
    width = down.shape[0] // 2 * HEAD
    return pl.pallas_call(
        hidden_kernel,
        grid_spec=pltpu.PrefetchScalarGridSpec(
            num_scalar_prefetch=1,
            grid=(steps,),
            in_specs=[
                pl.BlockSpec(parts.shape, lambda i, half: (0, 0, 0)),
                down_spec(down, steps),
            ],
            out_specs=[
                pl.BlockSpec((ROWS, units), lambda i, half: (0, 0)),
                pl.BlockSpec((ROWS, width // steps), lambda i, half: (0, i)),
            ],
        ),
        out_shape=(
            jax.ShapeDtypeStruct((ROWS, units), jnp.bfloat16),
            jax.ShapeDtypeStruct((ROWS, width), jnp.bfloat16),
        ),
        compiler_params=LIMIT,
        name="hidden_product",
    )(half, parts, down)


def down_kernel(half_ref, hidden_ref, down_ref, far_ref, near_ref):
    product = times_down(hidden_ref[...], down_ref) + far_ref[...].astype(jnp.float32)
    near_ref[...] = product.astype(jnp.bfloat16)


def down_product(half, hidden, down, far):
    steps = 4 if down.shape[0] % 8 == 0 else 1
    column = pl.BlockSpec((ROWS, far.shape[1] // steps), lambda i, half: (0, i))
    return pl.pallas_call(
        down_kernel,
        grid_spec=pltpu.PrefetchScalarGridSpec(
            num_scalar_prefetch=1,
            grid=(steps,),
            in_specs=[
                pl.BlockSpec(hidden.shape, lambda i, half: (0, 0)),
                down_spec(down, steps),
                column,
            ],
            out_specs=column,
        ),
        out_shape=jax.ShapeDtypeStruct(far.shape, jnp.bfloat16),
        compiler_params=LIMIT,
        name="down_product",
    )(half, hidden, down, far)


def swap(value):
    return lax.ppermute(value, "c", [(0, 1), (1, 0)])


def local(
    queries,
    fresh_kv,
    kv_pages,
    residual,
    norm_gain,
    out_weight,
    gate_weight,
    up_weight,
    down_weight,
    page_table,
    shared_pages,
    cache_lens,
    prefill_offsets,
):
    y_size, x_size, z_size = lax.axis_size("y"), lax.axis_size("x"), lax.axis_size("z")
    core = lax.axis_index("c")
    mine = lax.axis_index("z") * 2 + core
    near_half, far_half = core.reshape(1), (1 - core).reshape(1)
    own_rows = fresh_kv.shape[1]
    half = y_size // 2

    packed, own_kv, spread, limits = pack(
        x_size,
        cache_lens,
        prefill_offsets,
        jnp.transpose(page_table, (2, 0, 1)),
        shared_pages,
        (out_weight, gate_weight, up_weight),
        down_weight,
        kv_pages[0],
        fresh_kv[0],
    )
    weights = lax.all_gather(packed, "y", axis=0, tiled=True)
    far_kv = swap(own_kv)
    down = lax.all_to_all(spread, "x", 0, 0, tiled=True)
    parts, carried = attention(
        near_half, mine.reshape(1), own_rows, limits, residual, queries[0], own_kv, far_kv
    )
    parts, down = lax.optimization_barrier((parts, down))
    down = lax.all_gather(down, "y", axis=0, tiled=True)
    parts = lax.all_to_all(parts, "z", 0, 0, tiled=True)
    attended = lax.all_to_all(combine(parts, x_size), "x", 0, 0, tiled=True)
    attended = attended.reshape(x_size * ROWS, 2 * HEAD)

    far = swap(out_product(far_half, attended, weights))
    parts = out_product(near_half, attended, weights, far)
    parts = lax.all_to_all(parts, ("x", "z", "c"), 0, 0, tiled=True)
    parts = parts.reshape(x_size, z_size, 2, own_rows, half * HEAD)
    updated, sent = add_and_norm(parts, carried, norm_gain)
    near_rows = lax.all_to_all(
        sent.reshape(x_size * ROWS, half * HEAD), ("x", "z", "c"), 0, 0, tiled=True
    )
    far_rows = swap(near_rows)

    def partial(rows, which):
        piece = lax.dynamic_slice_in_dim(weights, which * half * HEAD, half * HEAD, 0)
        return jnp.dot(rows, piece[:, 2 * HEAD :], preferred_element_type=jnp.float32)

    gated = partial(near_rows, core) + partial(far_rows, 1 - core)
    gated, down = lax.optimization_barrier((gated.astype(jnp.bfloat16), down))
    gated = lax.all_to_all(gated, "x", 0, 0, tiled=True)
    gated = gated.reshape(x_size, ROWS, gated.shape[1])
    hidden, far = hidden_product(far_half, gated, down)
    parts = down_product(near_half, hidden, down, swap(far))
    parts = lax.all_to_all(parts, ("z", "c"), 0, 0, tiled=True)
    parts = parts.reshape(z_size, 2, own_rows, parts.shape[1])
    returned = jnp.transpose(jnp.sum(parts.astype(jnp.float32), axis=0), (1, 0, 2))
    return (updated + returned.reshape(own_rows, -1)).astype(jnp.bfloat16)[None]


def solution(mesh):
    cores = 2
    chips = mesh.shape["mlp"] // cores
    along = 4 if mesh.shape["grp"] % 16 == 0 else 2
    long_mesh = Mesh(
        mesh.devices.reshape(mesh.shape["grp"] // along, along, chips, cores), LONG
    )
    grp, mlp = ("y", "x"), ("z", "c")
    placed = (
        P(grp, None, None),
        P(grp, mlp, None),
        P(grp, mlp, None, None),
        P(grp, None, None),
        P(),
        P(mlp, grp),
        P(grp, mlp),
        P(grp, mlp),
        P(mlp, grp),
        P(grp, None, None),
        P(grp, None),
        P(grp, None),
        P(grp),
    )
    return jax.shard_map(
        local, mesh=long_mesh, in_specs=placed, out_specs=P(grp, mlp, None), check_vma=False
    )
```

```python
import functools

import jax
import jax.numpy as jnp
from jax import lax
from jax.experimental import pallas as pl
from jax.experimental.pallas import tpu as pltpu
from jax.sharding import Mesh
from jax.sharding import PartitionSpec as P

HEAD = 128
PAGE = 128
SHARED_PAGES = 4
PRIVATE_PAGES = 12
DECODES = 16
PREFILL = 112
ROWS = 128
OWN_PAGES = 2
FRESH_PAD = 16
KEYS = OWN_PAGES * PAGE + FRESH_PAD
STATS = 16
NEG_FILL = -1e30
EPSILON = 1e-05
LONG = "y", "x", "z", "c"
LIMIT = pltpu.CompilerParams(vmem_limit_bytes=32 * 1024 * 1024)
WIDE_LIMIT = pltpu.CompilerParams(vmem_limit_bytes=60 * 1024 * 1024)


def pieces(value):
    first = value.astype(jnp.bfloat16).astype(jnp.float32)
    rest = value - first
    second = rest.astype(jnp.bfloat16).astype(jnp.float32)
    return (first, second, rest - second)


def fill_limits(page_ids, lens_ref, offset_ref, table_ref, shared_ref, limit_ref):
    row = lax.broadcasted_iota(jnp.int32, (1, ROWS), 1)
    bound = jnp.full((1, ROWS), offset_ref[0], jnp.int32)
    for decode in range(DECODES):
        bound = jnp.where(row == PREFILL + decode, lens_ref[0, decode], bound)
    table, shared = table_ref[...], shared_ref[...]
    slot = lax.broadcasted_iota(jnp.int32, table.shape, 0)
    decode = lax.broadcasted_iota(jnp.int32, table.shape, 2) + 1
    shared_slot = lax.broadcasted_iota(jnp.int32, shared.shape, 1) + 1

    def whole(values):
        return jnp.sum(jnp.sum(values, axis=0), axis=1, keepdims=True)

    for index, page_id in enumerate(page_ids):
        listed = table == page_id
        owner = whole(jnp.where(listed, decode, 0)) - 1
        own_slot = whole(jnp.where(listed, slot, 0))
        prompt_slot = jnp.sum(
            jnp.where(shared == page_id, shared_slot, 0), axis=1, keepdims=True
        ) - 1
        prompt = jnp.broadcast_to(prompt_slot, row.shape) >= 0
        base = jnp.where(prompt_slot >= 0, prompt_slot, SHARED_PAGES + own_slot) * PAGE
        mine = (row >= PREFILL) & (row - PREFILL == owner)
        limit_ref[index : index + 1, :] = jnp.where(prompt | mine, bound - base, 0)


def attention_kernel(
    own_rows,
    core_ref,
    mine_ref,
    limit_ref,
    residual_ref,
    query_one,
    query_two,
    own_key,
    own_value,
    far_key,
    far_value,
    out_ref,
    carried_ref,
):
    @pl.when(pl.program_id(0) == 0)
    def _():
        carried_ref[...] = residual_ref[0].astype(jnp.float32)

    core = lax.axis_index("c")
    mine = 2 * lax.axis_index("z") + core
    sides = (mine, mine + 1 - 2 * core)
    query = jnp.concatenate(
        [query_one[:, :HEAD], query_one[:, HEAD:], query_two[:, :HEAD], query_two[:, HEAD:]], axis=0
    )
    keys = jnp.concatenate([own_key[...], far_key[...]], axis=0)
    values = jnp.concatenate([own_value[...], far_value[...]], axis=0)
    scores = lax.dot_general(
        keys, query, (((1,), (1,)), ((), ())), preferred_element_type=jnp.float32
    ) * (HEAD ** (-0.5))
    token = lax.broadcasted_iota(jnp.int32, (PAGE, ROWS), 0)
    fresh = lax.broadcasted_iota(jnp.int32, (FRESH_PAD, ROWS), 0)
    row = lax.broadcasted_iota(jnp.int32, (FRESH_PAD, ROWS), 1)
    seen = []
    for side in range(2):
        for page in range(OWN_PAGES):
            limit = limit_ref[pl.ds(side * OWN_PAGES + page, 1), :]
            seen.append((token < limit).astype(jnp.int32))
        key_row = sides[side] * own_rows + fresh
        before = jnp.where((key_row < PREFILL) & (key_row <= row), 1, 0)
        same = jnp.where(key_row == row, 1, 0)
        visible = jnp.where(row < PREFILL, before, same)
        seen.append(jnp.where(fresh < own_rows, visible, 0))
    seen = jnp.concatenate(seen, axis=0)
    seen = jnp.concatenate([seen] * 4, axis=1) > 0
    scores = jnp.where(seen, scores, NEG_FILL)
    peak = jnp.max(scores, axis=0, keepdims=True)
    exps = jnp.where(seen, jnp.exp(scores - peak), 0.0)
    total = jnp.sum(exps, axis=0, keepdims=True)
    mixed = lax.dot_general(
        values,
        exps.astype(jnp.bfloat16),
        (((0,), (0,)), ((), ())),
        preferred_element_type=jnp.float32,
    )
    line = lax.broadcasted_iota(jnp.int32, (STATS, ROWS), 0)
    for half in range(2):
        stats = jnp.zeros((STATS, ROWS), jnp.float32)
        for head in range(2):
            column = (2 * half + head) * ROWS
            out_ref[half, pl.ds(head * HEAD, HEAD), :] = mixed[:, column : column + ROWS].astype(
                jnp.bfloat16
            )
            sent = pieces(peak[:, column : column + ROWS]) + pieces(
                total[:, column : column + ROWS]
            )
            for index, value in enumerate(sent):
                stats = jnp.where(line == 6 * head + index, value, stats)
        out_ref[half, pl.ds(2 * HEAD, STATS), :] = stats.astype(jnp.bfloat16)


def attention(core, mine, own_rows, limits, residual, queries, own_kv, far_kv):
    kv_heads = own_kv.shape[1] // (2 * HEAD)
    chips = 2 * kv_heads
    width = residual.shape[2]

    def kv_spec(offset):
        return pl.BlockSpec((KEYS, HEAD), lambda j, core, mine: (0, offset + j))

    return pl.pallas_call(
        functools.partial(attention_kernel, own_rows),
        grid_spec=pltpu.PrefetchScalarGridSpec(
            num_scalar_prefetch=2,
            grid=(kv_heads,),
            in_specs=[
                pl.BlockSpec(limits.shape, lambda j, core, mine: (0, 0)),
                pl.BlockSpec((1, own_rows, width), lambda j, core, mine: (0, mine[0], 0)),
                pl.BlockSpec((ROWS, 2 * HEAD), lambda j, core, mine: (0, 4 * j + core[0])),
                pl.BlockSpec((ROWS, 2 * HEAD), lambda j, core, mine: (0, 4 * j + 2 + core[0])),
                kv_spec(0),
                kv_spec(kv_heads),
                kv_spec(0),
                kv_spec(kv_heads),
            ],
            out_specs=[
                pl.BlockSpec((2, 2 * HEAD + STATS, ROWS), lambda j, core, mine: (j, 0, 0)),
                pl.BlockSpec((own_rows, width), lambda j, core, mine: (0, 0)),
            ],
        ),
        out_shape=(
            jax.ShapeDtypeStruct((chips, 2 * HEAD + STATS, ROWS), jnp.bfloat16),
            jax.ShapeDtypeStruct((own_rows, width), jnp.float32),
        ),
        compiler_params=WIDE_LIMIT,
        name="attention",
    )(core, mine, limits, residual, queries, queries, own_kv, own_kv, far_kv, far_kv)


def combine_kernel(parts_ref, out_ref):
    chips = parts_ref.shape[0]
    for head in range(2):
        peaks = []
        totals = []
        for source in range(chips):
            stats = parts_ref[source, pl.ds(2 * HEAD, STATS), :].astype(jnp.float32)
            lines = [stats[6 * head + k : 6 * head + k + 1] for k in range(6)]
            peaks.append(lines[0] + lines[1] + lines[2])
            totals.append(lines[3] + lines[4] + lines[5])
        peak = peaks[0]
        for other in peaks[1:]:
            peak = jnp.maximum(peak, other)
        total = jnp.zeros_like(peak)
        mixed = jnp.zeros((HEAD, ROWS), jnp.float32)
        for source in range(chips):
            factor = jnp.exp(peaks[source] - peak)
            total = total + totals[source] * factor
            mixed = mixed + parts_ref[source, pl.ds(head * HEAD, HEAD), :].astype(jnp.float32) * factor
        attended = (mixed / total).T.astype(jnp.bfloat16)
        for copy in range(out_ref.shape[0]):
            out_ref[copy, :, head * HEAD : (head + 1) * HEAD] = attended


def combine(parts, copies):
    return pl.pallas_call(
        combine_kernel,
        out_shape=jax.ShapeDtypeStruct((copies, ROWS, 2 * HEAD), jnp.bfloat16),
        compiler_params=LIMIT,
        name="combine",
    )(parts)


def pack_kernel(
    lens_ref,
    offset_ref,
    table_ref,
    shared_ref,
    out_ref,
    gate_ref,
    up_ref,
    down_ref,
    pages_ref,
    fresh_ref,
    weights_ref,
    kv_ref,
    spread_ref,
    limit_ref,
):
    column = 0
    for source in (out_ref, gate_ref, up_ref):
        for row in range(0, source.shape[0], HEAD):
            width = source.shape[1]
            weights_ref[:, column : column + width] = source[row : row + HEAD, :]
            column += width
    for copy in range(spread_ref.shape[0]):
        spread_ref[copy] = down_ref[...]
    for page in range(OWN_PAGES):
        kv_ref[page * PAGE : (page + 1) * PAGE, :] = pages_ref[page]
    own_rows = fresh_ref.shape[0]
    rest = FRESH_PAD - own_rows
    fresh = fresh_ref[...]
    if rest:
        fresh = jnp.concatenate([fresh, jnp.zeros((rest, fresh.shape[1]), jnp.bfloat16)], axis=0)
    kv_ref[OWN_PAGES * PAGE :, :] = fresh
    core = lax.axis_index("c")
    mine = 2 * lax.axis_index("z") + core
    sides = (mine, mine + 1 - 2 * core)
    page_ids = [side * OWN_PAGES + page for side in sides for page in range(OWN_PAGES)]
    fill_limits(page_ids, lens_ref, offset_ref, table_ref, shared_ref, limit_ref)


def pack(copies, lens, offset, table, shared, weights, down_weight, pages, fresh):
    width = sum((piece.shape[0] // HEAD) * piece.shape[1] for piece in weights)
    smem = pl.BlockSpec(memory_space=pltpu.SMEM)
    vmem = pl.BlockSpec(memory_space=pltpu.VMEM)
    return pl.pallas_call(
        pack_kernel,
        in_specs=[smem] * 2 + [vmem] * 8,
        out_shape=(
            jax.ShapeDtypeStruct((HEAD, width), jnp.bfloat16),
            jax.ShapeDtypeStruct((KEYS, fresh.shape[1]), jnp.bfloat16),
            jax.ShapeDtypeStruct((copies,) + down_weight.shape, jnp.bfloat16),
            jax.ShapeDtypeStruct((2 * OWN_PAGES, ROWS), jnp.int32),
        ),
        compiler_params=WIDE_LIMIT,
        name="pack",
    )(lens, offset, table, shared, *weights, down_weight, pages, fresh)


def out_kernel(place_ref, attended_ref, weights_ref, *rest):
    result_ref = rest[-1]
    weights = jnp.concatenate([weights_ref[:, :HEAD], weights_ref[:, HEAD:]], axis=0)
    product = jnp.dot(attended_ref[...], weights, preferred_element_type=jnp.float32)
    if len(rest) == 2:
        product = product + rest[0][...].astype(jnp.float32)
    result_ref[...] = product.astype(jnp.bfloat16)


def out_product(half, attended, weights, far=None):
    rows = attended.shape[0]
    steps = weights.shape[0] // (2 * HEAD)
    column = pl.BlockSpec((rows, HEAD), lambda i, half: (0, i))
    return pl.pallas_call(
        out_kernel,
        grid_spec=pltpu.PrefetchScalarGridSpec(
            num_scalar_prefetch=1,
            grid=(steps,),
            in_specs=[
                pl.BlockSpec((rows, 2 * HEAD), lambda i, half: (0, 0)),
                pl.BlockSpec((HEAD, 2 * HEAD), lambda i, half: (half[0] * steps + i, 0)),
            ]
            + ([] if far is None else [column]),
            out_specs=column,
        ),
        out_shape=jax.ShapeDtypeStruct((rows, steps * HEAD), jnp.bfloat16),
        compiler_params=LIMIT,
        name="out_product",
    )(half, attended, weights, *(() if far is None else (far,)))


def norm_kernel(parts_ref, residual_ref, gain_ref, updated_ref, sent_ref):
    x_size, z_size = parts_ref.shape[:2]
    blocks = parts_ref.shape[4] // HEAD
    square = jnp.zeros((parts_ref.shape[3], 1), jnp.float32)
    for x in range(x_size):
        for core in range(2):
            summed = parts_ref[x, 0, core].astype(jnp.float32)
            for z in range(1, z_size):
                summed = summed + parts_ref[x, z, core].astype(jnp.float32)
            for block in range(blocks):
                column = ((core * blocks + block) * x_size + x) * HEAD
                value = summed[:, block * HEAD : (block + 1) * HEAD]
                value = value + residual_ref[:, column : column + HEAD]
                square = square + jnp.sum(value * value, axis=1, keepdims=True)
                updated_ref[:, column : column + HEAD] = value
    scale = lax.rsqrt(square / (2 * x_size * blocks * HEAD) + EPSILON)
    for x in range(x_size):
        for core in range(2):
            normed = []
            for block in range(blocks):
                column = ((core * blocks + block) * x_size + x) * HEAD
                value = updated_ref[:, column : column + HEAD] * scale
                normed.append(value * gain_ref[:, column : column + HEAD])
            normed = jnp.concatenate(normed, axis=1).astype(jnp.bfloat16)
            for z in range(z_size):
                sent_ref[x, z, core] = normed


def add_and_norm(parts, residual, gain):
    return pl.pallas_call(
        norm_kernel,
        out_shape=(
            jax.ShapeDtypeStruct(residual.shape, jnp.float32),
            jax.ShapeDtypeStruct(parts.shape, jnp.bfloat16),
        ),
        compiler_params=LIMIT,
        name="add_and_norm",
    )(parts, residual, gain.reshape(1, -1))


def gate_kernel(near_ref, far_ref, near_rows, far_rows, near_weights, far_weights, gated_ref):
    product = jnp.dot(near_rows[...], near_weights[...], preferred_element_type=jnp.float32)
    product = product + jnp.dot(
        far_rows[...], far_weights[...], preferred_element_type=jnp.float32
    )
    gated_ref[...] = product.astype(jnp.bfloat16)


def gate_product(near_half, far_half, near_rows, far_rows, weights):
    rows, depth = near_rows.shape
    tile = 2 * HEAD
    steps = weights.shape[1] // tile - 1
    whole = pl.BlockSpec((rows, depth), lambda i, near, far: (0, 0))
    return pl.pallas_call(
        gate_kernel,
        grid_spec=pltpu.PrefetchScalarGridSpec(
            num_scalar_prefetch=2,
            grid=(steps,),
            in_specs=[
                whole,
                whole,
                pl.BlockSpec((depth, tile), lambda i, near, far: (near[0], 1 + i)),
                pl.BlockSpec((depth, tile), lambda i, near, far: (far[0], 1 + i)),
            ],
            out_specs=pl.BlockSpec((rows, tile), lambda i, near, far: (0, i)),
        ),
        out_shape=jax.ShapeDtypeStruct((rows, steps * tile), jnp.bfloat16),
        compiler_params=LIMIT,
        name="gate_product",
    )(near_half, far_half, near_rows, far_rows, weights, weights)


def times_down(hidden, down_ref):
    return jnp.concatenate(
        [
            jnp.dot(hidden, down_ref[block], preferred_element_type=jnp.float32)
            for block in range(down_ref.shape[0])
        ],
        axis=1,
    )


def hidden_kernel(half_ref, parts_ref, down_ref, hidden_ref, far_ref):
    @pl.when(pl.program_id(0) == 0)
    def _():
        summed = parts_ref[0].astype(jnp.float32)
        for source in range(1, parts_ref.shape[0]):
            summed = summed + parts_ref[source].astype(jnp.float32)
        units = summed.shape[1] // 2
        gate = summed[:, :units]
        hidden_ref[...] = (gate / (1.0 + jnp.exp(-gate)) * summed[:, units:]).astype(jnp.bfloat16)

    far_ref[...] = times_down(hidden_ref[...], down_ref).astype(jnp.bfloat16)


def down_spec(down, steps):
    blocks = down.shape[0] // (2 * steps)
    return pl.BlockSpec((blocks,) + down.shape[1:], lambda i, half: (half[0] * steps + i, 0, 0))


def hidden_product(half, parts, down):
    units = down.shape[1]
    steps = 4 if down.shape[0] % 8 == 0 else 1
    width = down.shape[0] // 2 * HEAD
    return pl.pallas_call(
        hidden_kernel,
        grid_spec=pltpu.PrefetchScalarGridSpec(
            num_scalar_prefetch=1,
            grid=(steps,),
            in_specs=[
                pl.BlockSpec(parts.shape, lambda i, half: (0, 0, 0)),
                down_spec(down, steps),
            ],
            out_specs=[
                pl.BlockSpec((ROWS, units), lambda i, half: (0, 0)),
                pl.BlockSpec((ROWS, width // steps), lambda i, half: (0, i)),
            ],
        ),
        out_shape=(
            jax.ShapeDtypeStruct((ROWS, units), jnp.bfloat16),
            jax.ShapeDtypeStruct((ROWS, width), jnp.bfloat16),
        ),
        compiler_params=LIMIT,
        name="hidden_product",
    )(half, parts, down)


def down_kernel(half_ref, hidden_ref, down_ref, far_ref, near_ref):
    product = times_down(hidden_ref[...], down_ref) + far_ref[...].astype(jnp.float32)
    near_ref[...] = product.astype(jnp.bfloat16)


def down_product(half, hidden, down, far):
    steps = 4 if down.shape[0] % 8 == 0 else 1
    column = pl.BlockSpec((ROWS, far.shape[1] // steps), lambda i, half: (0, i))
    return pl.pallas_call(
        down_kernel,
        grid_spec=pltpu.PrefetchScalarGridSpec(
            num_scalar_prefetch=1,
            grid=(steps,),
            in_specs=[
                pl.BlockSpec(hidden.shape, lambda i, half: (0, 0)),
                down_spec(down, steps),
                column,
            ],
            out_specs=column,
        ),
        out_shape=jax.ShapeDtypeStruct(far.shape, jnp.bfloat16),
        compiler_params=LIMIT,
        name="down_product",
    )(half, hidden, down, far)


def swap(value):
    return lax.ppermute(value, "c", [(0, 1), (1, 0)])


def local(
    queries,
    fresh_kv,
    kv_pages,
    residual,
    norm_gain,
    out_weight,
    gate_weight,
    up_weight,
    down_weight,
    page_table,
    shared_pages,
    cache_lens,
    prefill_offsets,
):
    y_size, x_size, z_size = lax.axis_size("y"), lax.axis_size("x"), lax.axis_size("z")
    core = lax.axis_index("c")
    mine = lax.axis_index("z") * 2 + core
    near_half, far_half = core.reshape(1), (1 - core).reshape(1)
    own_rows = fresh_kv.shape[1]
    half = y_size // 2

    packed, own_kv, spread, limits = pack(
        x_size,
        cache_lens,
        prefill_offsets,
        jnp.transpose(page_table, (2, 0, 1)),
        shared_pages,
        (out_weight, gate_weight, up_weight),
        down_weight,
        kv_pages[0],
        fresh_kv[0],
    )
    weights = lax.all_gather(packed, "y", axis=0, tiled=True)
    far_kv = swap(own_kv)
    down = lax.all_to_all(spread, "x", 0, 0, tiled=True)
    parts, carried = attention(
        near_half, mine.reshape(1), own_rows, limits, residual, queries[0], own_kv, far_kv
    )
    parts, down = lax.optimization_barrier((parts, down))
    down = lax.all_gather(down, "y", axis=0, tiled=True)
    parts = lax.all_to_all(parts, "z", 0, 0, tiled=True)
    attended = lax.all_to_all(combine(parts, x_size), "x", 0, 0, tiled=True)
    attended = attended.reshape(x_size * ROWS, 2 * HEAD)

    columns = weights[:, : 2 * HEAD]
    far = swap(out_product(far_half, attended, columns))
    parts = out_product(near_half, attended, columns, far)
    parts = lax.all_to_all(parts, ("x", "z", "c"), 0, 0, tiled=True)
    parts = parts.reshape(x_size, z_size, 2, own_rows, half * HEAD)
    updated, sent = add_and_norm(parts, carried, norm_gain)
    near_rows = lax.all_to_all(
        sent.reshape(x_size * ROWS, half * HEAD), ("x", "z", "c"), 0, 0, tiled=True
    )
    far_rows, down = lax.optimization_barrier((swap(near_rows), down))

    gated = gate_product(near_half, far_half, near_rows, far_rows, weights)
    gated = lax.all_to_all(gated, "x", 0, 0, tiled=True)
    gated = gated.reshape(x_size, ROWS, gated.shape[1])
    hidden, far = hidden_product(far_half, gated, down)
    parts = down_product(near_half, hidden, down, swap(far))
    parts = lax.all_to_all(parts, ("z", "c"), 0, 0, tiled=True)
    parts = parts.reshape(z_size, 2, own_rows, parts.shape[1])
    returned = jnp.transpose(jnp.sum(parts.astype(jnp.float32), axis=0), (1, 0, 2))
    return (updated + returned.reshape(own_rows, -1)).astype(jnp.bfloat16)[None]


def solution(mesh):
    cores = 2
    chips = mesh.shape["mlp"] // cores
    along = 4 if mesh.shape["grp"] % 16 == 0 else 2
    long_mesh = Mesh(
        mesh.devices.reshape(mesh.shape["grp"] // along, along, chips, cores), LONG
    )
    grp, mlp = ("y", "x"), ("z", "c")
    placed = (
        P(grp, None, None),
        P(grp, mlp, None),
        P(grp, mlp, None, None),
        P(grp, None, None),
        P(),
        P(mlp, grp),
        P(grp, mlp),
        P(grp, mlp),
        P(mlp, grp),
        P(grp, None, None),
        P(grp, None),
        P(grp, None),
        P(grp),
    )
    return jax.shard_map(
        local, mesh=long_mesh, in_specs=placed, out_specs=P(grp, mlp, None), check_vma=False
    )
```

```python
import functools

import jax
import jax.numpy as jnp
from jax import lax
from jax.experimental import pallas as pl
from jax.experimental.pallas import tpu as pltpu
from jax.sharding import Mesh
from jax.sharding import PartitionSpec as P

HEAD = 128
PAGE = 128
SHARED_PAGES = 4
PRIVATE_PAGES = 12
DECODES = 16
PREFILL = 112
ROWS = 128
OWN_PAGES = 2
FRESH_PAD = 16
KEYS = OWN_PAGES * PAGE + FRESH_PAD
STATS = 16
NEG_FILL = -1e30
EPSILON = 1e-05
LONG = "y", "x", "z", "c"
LIMIT = pltpu.CompilerParams(vmem_limit_bytes=32 * 1024 * 1024)
WIDE_LIMIT = pltpu.CompilerParams(vmem_limit_bytes=60 * 1024 * 1024)


def pieces(value):
    first = value.astype(jnp.bfloat16).astype(jnp.float32)
    rest = value - first
    second = rest.astype(jnp.bfloat16).astype(jnp.float32)
    return (first, second, rest - second)


def fill_limits(page_ids, lens_ref, offset_ref, table_ref, shared_ref, limit_ref):
    row = lax.broadcasted_iota(jnp.int32, (1, ROWS), 1)
    bound = jnp.full((1, ROWS), offset_ref[0], jnp.int32)
    for decode in range(DECODES):
        bound = jnp.where(row == PREFILL + decode, lens_ref[0, decode], bound)
    table, shared = table_ref[...], shared_ref[...]
    slot = lax.broadcasted_iota(jnp.int32, table.shape, 0)
    decode = lax.broadcasted_iota(jnp.int32, table.shape, 2) + 1
    shared_slot = lax.broadcasted_iota(jnp.int32, shared.shape, 1) + 1

    def whole(values):
        return jnp.sum(jnp.sum(values, axis=0), axis=1, keepdims=True)

    for index, page_id in enumerate(page_ids):
        listed = table == page_id
        owner = whole(jnp.where(listed, decode, 0)) - 1
        own_slot = whole(jnp.where(listed, slot, 0))
        prompt_slot = jnp.sum(
            jnp.where(shared == page_id, shared_slot, 0), axis=1, keepdims=True
        ) - 1
        prompt = jnp.broadcast_to(prompt_slot, row.shape) >= 0
        base = jnp.where(prompt_slot >= 0, prompt_slot, SHARED_PAGES + own_slot) * PAGE
        mine = (row >= PREFILL) & (row - PREFILL == owner)
        limit_ref[index : index + 1, :] = jnp.where(prompt | mine, bound - base, 0)


def attention_kernel(
    own_rows,
    core_ref,
    mine_ref,
    limit_ref,
    residual_ref,
    query_one,
    query_two,
    own_key,
    own_value,
    far_key,
    far_value,
    out_ref,
    carried_ref,
):
    @pl.when(pl.program_id(0) == 0)
    def _():
        carried_ref[...] = residual_ref[0].astype(jnp.float32)

    core = lax.axis_index("c")
    mine = 2 * lax.axis_index("z") + core
    sides = (mine, mine + 1 - 2 * core)
    query = jnp.concatenate(
        [query_one[:, :HEAD], query_one[:, HEAD:], query_two[:, :HEAD], query_two[:, HEAD:]], axis=0
    )
    keys = jnp.concatenate([own_key[...], far_key[...]], axis=0)
    values = jnp.concatenate([own_value[...], far_value[...]], axis=0)
    scores = lax.dot_general(
        keys, query, (((1,), (1,)), ((), ())), preferred_element_type=jnp.float32
    ) * (HEAD ** (-0.5))
    token = lax.broadcasted_iota(jnp.int32, (PAGE, ROWS), 0)
    fresh = lax.broadcasted_iota(jnp.int32, (FRESH_PAD, ROWS), 0)
    row = lax.broadcasted_iota(jnp.int32, (FRESH_PAD, ROWS), 1)
    seen = []
    for side in range(2):
        for page in range(OWN_PAGES):
            limit = limit_ref[pl.ds(side * OWN_PAGES + page, 1), :]
            seen.append((token < limit).astype(jnp.int32))
        key_row = sides[side] * own_rows + fresh
        before = jnp.where((key_row < PREFILL) & (key_row <= row), 1, 0)
        same = jnp.where(key_row == row, 1, 0)
        visible = jnp.where(row < PREFILL, before, same)
        seen.append(jnp.where(fresh < own_rows, visible, 0))
    seen = jnp.concatenate(seen, axis=0)
    seen = jnp.concatenate([seen] * 4, axis=1) > 0
    scores = jnp.where(seen, scores, NEG_FILL)
    peak = jnp.max(scores, axis=0, keepdims=True)
    exps = jnp.where(seen, jnp.exp(scores - peak), 0.0)
    total = jnp.sum(exps, axis=0, keepdims=True)
    mixed = lax.dot_general(
        values,
        exps.astype(jnp.bfloat16),
        (((0,), (0,)), ((), ())),
        preferred_element_type=jnp.float32,
    )
    line = lax.broadcasted_iota(jnp.int32, (STATS, ROWS), 0)
    for half in range(2):
        stats = jnp.zeros((STATS, ROWS), jnp.float32)
        for head in range(2):
            column = (2 * half + head) * ROWS
            out_ref[half, pl.ds(head * HEAD, HEAD), :] = mixed[:, column : column + ROWS].astype(
                jnp.bfloat16
            )
            sent = pieces(peak[:, column : column + ROWS]) + pieces(
                total[:, column : column + ROWS]
            )
            for index, value in enumerate(sent):
                stats = jnp.where(line == 6 * head + index, value, stats)
        out_ref[half, pl.ds(2 * HEAD, STATS), :] = stats.astype(jnp.bfloat16)


def attention(core, mine, own_rows, limits, residual, queries, own_kv, far_kv):
    kv_heads = own_kv.shape[1] // (2 * HEAD)
    chips = 2 * kv_heads
    width = residual.shape[2]

    def kv_spec(offset):
        return pl.BlockSpec((KEYS, HEAD), lambda j, core, mine: (0, offset + j))

    return pl.pallas_call(
        functools.partial(attention_kernel, own_rows),
        grid_spec=pltpu.PrefetchScalarGridSpec(
            num_scalar_prefetch=2,
            grid=(kv_heads,),
            in_specs=[
                pl.BlockSpec(limits.shape, lambda j, core, mine: (0, 0)),
                pl.BlockSpec((1, own_rows, width), lambda j, core, mine: (0, mine[0], 0)),
                pl.BlockSpec((ROWS, 2 * HEAD), lambda j, core, mine: (0, 4 * j + core[0])),
                pl.BlockSpec((ROWS, 2 * HEAD), lambda j, core, mine: (0, 4 * j + 2 + core[0])),
                kv_spec(0),
                kv_spec(kv_heads),
                kv_spec(0),
                kv_spec(kv_heads),
            ],
            out_specs=[
                pl.BlockSpec((2, 2 * HEAD + STATS, ROWS), lambda j, core, mine: (j, 0, 0)),
                pl.BlockSpec((own_rows, width), lambda j, core, mine: (0, 0)),
            ],
        ),
        out_shape=(
            jax.ShapeDtypeStruct((chips, 2 * HEAD + STATS, ROWS), jnp.bfloat16),
            jax.ShapeDtypeStruct((own_rows, width), jnp.float32),
        ),
        compiler_params=WIDE_LIMIT,
        name="attention",
    )(core, mine, limits, residual, queries, queries, own_kv, own_kv, far_kv, far_kv)


def combine_kernel(parts_ref, out_ref):
    chips = parts_ref.shape[0]
    for head in range(2):
        peaks = []
        totals = []
        for source in range(chips):
            stats = parts_ref[source, pl.ds(2 * HEAD, STATS), :].astype(jnp.float32)
            lines = [stats[6 * head + k : 6 * head + k + 1] for k in range(6)]
            peaks.append(lines[0] + lines[1] + lines[2])
            totals.append(lines[3] + lines[4] + lines[5])
        peak = peaks[0]
        for other in peaks[1:]:
            peak = jnp.maximum(peak, other)
        total = jnp.zeros_like(peak)
        mixed = jnp.zeros((HEAD, ROWS), jnp.float32)
        for source in range(chips):
            factor = jnp.exp(peaks[source] - peak)
            total = total + totals[source] * factor
            mixed = mixed + parts_ref[source, pl.ds(head * HEAD, HEAD), :].astype(jnp.float32) * factor
        attended = (mixed / total).T.astype(jnp.bfloat16)
        for copy in range(out_ref.shape[0]):
            out_ref[copy, :, head * HEAD : (head + 1) * HEAD] = attended


def combine(parts, copies):
    return pl.pallas_call(
        combine_kernel,
        out_shape=jax.ShapeDtypeStruct((copies, ROWS, 2 * HEAD), jnp.bfloat16),
        compiler_params=LIMIT,
        name="combine",
    )(parts)


def pack_kernel(
    lens_ref,
    offset_ref,
    table_ref,
    shared_ref,
    out_ref,
    gate_ref,
    up_ref,
    down_ref,
    pages_ref,
    fresh_ref,
    weights_ref,
    kv_ref,
    spread_ref,
    limit_ref,
):
    column = 0
    for source in (out_ref, gate_ref, up_ref):
        for row in range(0, source.shape[0], HEAD):
            width = source.shape[1]
            weights_ref[:, column : column + width] = source[row : row + HEAD, :]
            column += width
    for copy in range(spread_ref.shape[0]):
        spread_ref[copy] = down_ref[...]
    for page in range(OWN_PAGES):
        kv_ref[page * PAGE : (page + 1) * PAGE, :] = pages_ref[page]
    own_rows = fresh_ref.shape[0]
    rest = FRESH_PAD - own_rows
    fresh = fresh_ref[...]
    if rest:
        fresh = jnp.concatenate([fresh, jnp.zeros((rest, fresh.shape[1]), jnp.bfloat16)], axis=0)
    kv_ref[OWN_PAGES * PAGE :, :] = fresh
    core = lax.axis_index("c")
    mine = 2 * lax.axis_index("z") + core
    sides = (mine, mine + 1 - 2 * core)
    page_ids = [side * OWN_PAGES + page for side in sides for page in range(OWN_PAGES)]
    fill_limits(page_ids, lens_ref, offset_ref, table_ref, shared_ref, limit_ref)


def pack(copies, lens, offset, table, shared, weights, down_weight, pages, fresh):
    width = sum((piece.shape[0] // HEAD) * piece.shape[1] for piece in weights)
    smem = pl.BlockSpec(memory_space=pltpu.SMEM)
    vmem = pl.BlockSpec(memory_space=pltpu.VMEM)
    return pl.pallas_call(
        pack_kernel,
        in_specs=[smem] * 2 + [vmem] * 8,
        out_shape=(
            jax.ShapeDtypeStruct((HEAD, width), jnp.bfloat16),
            jax.ShapeDtypeStruct((KEYS, fresh.shape[1]), jnp.bfloat16),
            jax.ShapeDtypeStruct((copies,) + down_weight.shape, jnp.bfloat16),
            jax.ShapeDtypeStruct((2 * OWN_PAGES, ROWS), jnp.int32),
        ),
        compiler_params=WIDE_LIMIT,
        name="pack",
    )(lens, offset, table, shared, *weights, down_weight, pages, fresh)


def out_kernel(place_ref, attended_ref, weights_ref, *rest):
    result_ref = rest[-1]
    weights = jnp.concatenate([weights_ref[:, :HEAD], weights_ref[:, HEAD:]], axis=0)
    product = jnp.dot(attended_ref[...], weights, preferred_element_type=jnp.float32)
    if len(rest) == 2:
        product = product + rest[0][...].astype(jnp.float32)
    result_ref[...] = product.astype(jnp.bfloat16)


def out_product(half, attended, weights, far=None):
    rows = attended.shape[0]
    steps = weights.shape[0] // (2 * HEAD)
    column = pl.BlockSpec((rows, HEAD), lambda i, half: (0, i))
    return pl.pallas_call(
        out_kernel,
        grid_spec=pltpu.PrefetchScalarGridSpec(
            num_scalar_prefetch=1,
            grid=(steps,),
            in_specs=[
                pl.BlockSpec((rows, 2 * HEAD), lambda i, half: (0, 0)),
                pl.BlockSpec((HEAD, 2 * HEAD), lambda i, half: (half[0] * steps + i, 0)),
            ]
            + ([] if far is None else [column]),
            out_specs=column,
        ),
        out_shape=jax.ShapeDtypeStruct((rows, steps * HEAD), jnp.bfloat16),
        compiler_params=LIMIT,
        name="out_product",
    )(half, attended, weights, *(() if far is None else (far,)))


def norm_kernel(parts_ref, residual_ref, gain_ref, updated_ref, sent_ref):
    x_size, z_size = parts_ref.shape[:2]
    blocks = parts_ref.shape[4] // HEAD
    square = jnp.zeros((parts_ref.shape[3], 1), jnp.float32)
    for x in range(x_size):
        for core in range(2):
            summed = parts_ref[x, 0, core].astype(jnp.float32)
            for z in range(1, z_size):
                summed = summed + parts_ref[x, z, core].astype(jnp.float32)
            for block in range(blocks):
                column = ((core * blocks + block) * x_size + x) * HEAD
                value = summed[:, block * HEAD : (block + 1) * HEAD]
                value = value + residual_ref[:, column : column + HEAD]
                square = square + jnp.sum(value * value, axis=1, keepdims=True)
                updated_ref[:, column : column + HEAD] = value
    scale = lax.rsqrt(square / (2 * x_size * blocks * HEAD) + EPSILON)
    for x in range(x_size):
        for core in range(2):
            normed = []
            for block in range(blocks):
                column = ((core * blocks + block) * x_size + x) * HEAD
                value = updated_ref[:, column : column + HEAD] * scale
                normed.append(value * gain_ref[:, column : column + HEAD])
            normed = jnp.concatenate(normed, axis=1).astype(jnp.bfloat16)
            for z in range(z_size):
                sent_ref[x, z, core] = normed


def add_and_norm(parts, residual, gain):
    return pl.pallas_call(
        norm_kernel,
        out_shape=(
            jax.ShapeDtypeStruct(residual.shape, jnp.float32),
            jax.ShapeDtypeStruct(parts.shape, jnp.bfloat16),
        ),
        compiler_params=LIMIT,
        name="add_and_norm",
    )(parts, residual, gain.reshape(1, -1))


def gate_kernel(near_ref, far_ref, near_rows, far_rows, near_weights, far_weights, gated_ref):
    product = jnp.dot(near_rows[...], near_weights[...], preferred_element_type=jnp.float32)
    product = product + jnp.dot(
        far_rows[...], far_weights[...], preferred_element_type=jnp.float32
    )
    gated_ref[...] = product.astype(jnp.bfloat16)


def gate_product(near_half, far_half, near_rows, far_rows, weights):
    rows, depth = near_rows.shape
    tile = 2 * HEAD
    steps = weights.shape[1] // tile - 1
    whole = pl.BlockSpec((rows, depth), lambda i, near, far: (0, 0))
    return pl.pallas_call(
        gate_kernel,
        grid_spec=pltpu.PrefetchScalarGridSpec(
            num_scalar_prefetch=2,
            grid=(steps,),
            in_specs=[
                whole,
                whole,
                pl.BlockSpec((depth, tile), lambda i, near, far: (near[0], 1 + i)),
                pl.BlockSpec((depth, tile), lambda i, near, far: (far[0], 1 + i)),
            ],
            out_specs=pl.BlockSpec((rows, tile), lambda i, near, far: (0, i)),
        ),
        out_shape=jax.ShapeDtypeStruct((rows, steps * tile), jnp.bfloat16),
        compiler_params=LIMIT,
        name="gate_product",
    )(near_half, far_half, near_rows, far_rows, weights, weights)


def times_down(hidden, down_ref):
    return jnp.concatenate(
        [
            jnp.dot(hidden, down_ref[block], preferred_element_type=jnp.float32)
            for block in range(down_ref.shape[0])
        ],
        axis=1,
    )


def hidden_kernel(half_ref, parts_ref, down_ref, hidden_ref, far_ref):
    @pl.when(pl.program_id(0) == 0)
    def _():
        summed = parts_ref[0].astype(jnp.float32)
        for source in range(1, parts_ref.shape[0]):
            summed = summed + parts_ref[source].astype(jnp.float32)
        units = summed.shape[1] // 2
        gate = summed[:, :units]
        hidden_ref[...] = (gate / (1.0 + jnp.exp(-gate)) * summed[:, units:]).astype(jnp.bfloat16)

    far_ref[...] = times_down(hidden_ref[...], down_ref).astype(jnp.bfloat16)


def down_spec(down, steps):
    blocks = down.shape[0] // (2 * steps)
    return pl.BlockSpec((blocks,) + down.shape[1:], lambda i, half: (half[0] * steps + i, 0, 0))


def hidden_product(half, parts, down):
    units = down.shape[1]
    steps = 4 if down.shape[0] % 8 == 0 else 1
    width = down.shape[0] // 2 * HEAD
    return pl.pallas_call(
        hidden_kernel,
        grid_spec=pltpu.PrefetchScalarGridSpec(
            num_scalar_prefetch=1,
            grid=(steps,),
            in_specs=[
                pl.BlockSpec(parts.shape, lambda i, half: (0, 0, 0)),
                down_spec(down, steps),
            ],
            out_specs=[
                pl.BlockSpec((ROWS, units), lambda i, half: (0, 0)),
                pl.BlockSpec((ROWS, width // steps), lambda i, half: (0, i)),
            ],
        ),
        out_shape=(
            jax.ShapeDtypeStruct((ROWS, units), jnp.bfloat16),
            jax.ShapeDtypeStruct((ROWS, width), jnp.bfloat16),
        ),
        compiler_params=LIMIT,
        name="hidden_product",
    )(half, parts, down)


def down_kernel(half_ref, hidden_ref, down_ref, far_ref, near_ref):
    product = times_down(hidden_ref[...], down_ref) + far_ref[...].astype(jnp.float32)
    near_ref[...] = product.astype(jnp.bfloat16)


def down_product(half, hidden, down, far):
    steps = 4 if down.shape[0] % 8 == 0 else 1
    column = pl.BlockSpec((ROWS, far.shape[1] // steps), lambda i, half: (0, i))
    return pl.pallas_call(
        down_kernel,
        grid_spec=pltpu.PrefetchScalarGridSpec(
            num_scalar_prefetch=1,
            grid=(steps,),
            in_specs=[
                pl.BlockSpec(hidden.shape, lambda i, half: (0, 0)),
                down_spec(down, steps),
                column,
            ],
            out_specs=column,
        ),
        out_shape=jax.ShapeDtypeStruct(far.shape, jnp.bfloat16),
        compiler_params=LIMIT,
        name="down_product",
    )(half, hidden, down, far)


def swap(value):
    return lax.ppermute(value, "c", [(0, 1), (1, 0)])


def local(
    queries,
    fresh_kv,
    kv_pages,
    residual,
    norm_gain,
    out_weight,
    gate_weight,
    up_weight,
    down_weight,
    page_table,
    shared_pages,
    cache_lens,
    prefill_offsets,
):
    y_size, x_size, z_size = lax.axis_size("y"), lax.axis_size("x"), lax.axis_size("z")
    core = lax.axis_index("c")
    mine = lax.axis_index("z") * 2 + core
    near_half, far_half = core.reshape(1), (1 - core).reshape(1)
    own_rows = fresh_kv.shape[1]
    half = y_size // 2

    packed, own_kv, spread, limits = pack(
        x_size,
        cache_lens,
        prefill_offsets,
        jnp.transpose(page_table, (2, 0, 1)),
        shared_pages,
        (out_weight, gate_weight, up_weight),
        down_weight,
        kv_pages[0],
        fresh_kv[0],
    )
    weights = lax.all_gather(packed, "y", axis=0, tiled=True)
    far_kv = swap(own_kv)
    down = lax.all_to_all(spread, "x", 0, 0, tiled=True)
    parts, carried = attention(
        near_half, mine.reshape(1), own_rows, limits, residual, queries[0], own_kv, far_kv
    )
    parts, down = lax.optimization_barrier((parts, down))
    parts = lax.all_to_all(parts, "z", 0, 0, tiled=True)
    combined = combine(parts, x_size)
    down, _ = lax.optimization_barrier((down, combined))
    down = lax.all_gather(down, "y", axis=0, tiled=True)
    attended = lax.all_to_all(combined, "x", 0, 0, tiled=True)
    attended = attended.reshape(x_size * ROWS, 2 * HEAD)

    columns = weights[:, : 2 * HEAD]
    far = swap(out_product(far_half, attended, columns))
    parts = out_product(near_half, attended, columns, far)
    parts = lax.all_to_all(parts, ("x", "z", "c"), 0, 0, tiled=True)
    parts = parts.reshape(x_size, z_size, 2, own_rows, half * HEAD)
    updated, sent = add_and_norm(parts, carried, norm_gain)
    near_rows = lax.all_to_all(
        sent.reshape(x_size * ROWS, half * HEAD), ("x", "z", "c"), 0, 0, tiled=True
    )
    far_rows, down = lax.optimization_barrier((swap(near_rows), down))

    gated = gate_product(near_half, far_half, near_rows, far_rows, weights)
    gated = lax.all_to_all(gated, "x", 0, 0, tiled=True)
    gated = gated.reshape(x_size, ROWS, gated.shape[1])
    hidden, far = hidden_product(far_half, gated, down)
    parts = down_product(near_half, hidden, down, swap(far))
    parts = lax.all_to_all(parts, ("z", "c"), 0, 0, tiled=True)
    parts = parts.reshape(z_size, 2, own_rows, parts.shape[1])
    returned = jnp.transpose(jnp.sum(parts.astype(jnp.float32), axis=0), (1, 0, 2))
    return (updated + returned.reshape(own_rows, -1)).astype(jnp.bfloat16)[None]


def solution(mesh):
    cores = 2
    chips = mesh.shape["mlp"] // cores
    along = 4 if mesh.shape["grp"] % 16 == 0 else 2
    long_mesh = Mesh(
        mesh.devices.reshape(mesh.shape["grp"] // along, along, chips, cores), LONG
    )
    grp, mlp = ("y", "x"), ("z", "c")
    placed = (
        P(grp, None, None),
        P(grp, mlp, None),
        P(grp, mlp, None, None),
        P(grp, None, None),
        P(),
        P(mlp, grp),
        P(grp, mlp),
        P(grp, mlp),
        P(mlp, grp),
        P(grp, None, None),
        P(grp, None),
        P(grp, None),
        P(grp),
    )
    return jax.shard_map(
        local, mesh=long_mesh, in_specs=placed, out_specs=P(grp, mlp, None), check_vma=False
    )
```

```python
import functools

import jax
import jax.numpy as jnp
from jax import lax
from jax.experimental import pallas as pl
from jax.experimental.pallas import tpu as pltpu
from jax.sharding import Mesh
from jax.sharding import PartitionSpec as P

HEAD = 128
PAGE = 128
SHARED_PAGES = 4
PRIVATE_PAGES = 12
DECODES = 16
PREFILL = 112
ROWS = 128
OWN_PAGES = 2
FRESH_PAD = 16
KEYS = OWN_PAGES * PAGE + FRESH_PAD
STATS = 16
NEG_FILL = -1e30
EPSILON = 1e-05
LONG = "y", "x", "z", "c"
LIMIT = pltpu.CompilerParams(vmem_limit_bytes=32 * 1024 * 1024)
WIDE_LIMIT = pltpu.CompilerParams(vmem_limit_bytes=60 * 1024 * 1024)


def pieces(value):
    first = value.astype(jnp.bfloat16).astype(jnp.float32)
    rest = value - first
    second = rest.astype(jnp.bfloat16).astype(jnp.float32)
    return (first, second, rest - second)


def fill_limits(page_ids, lens_ref, offset_ref, table_ref, shared_ref, limit_ref):
    row = lax.broadcasted_iota(jnp.int32, (1, ROWS), 1)
    bound = jnp.full((1, ROWS), offset_ref[0], jnp.int32)
    for decode in range(DECODES):
        bound = jnp.where(row == PREFILL + decode, lens_ref[0, decode], bound)
    table, shared = table_ref[...], shared_ref[...]
    slot = lax.broadcasted_iota(jnp.int32, table.shape, 0)
    decode = lax.broadcasted_iota(jnp.int32, table.shape, 2) + 1
    shared_slot = lax.broadcasted_iota(jnp.int32, shared.shape, 1) + 1

    def whole(values):
        return jnp.sum(jnp.sum(values, axis=0), axis=1, keepdims=True)

    for index, page_id in enumerate(page_ids):
        listed = table == page_id
        owner = whole(jnp.where(listed, decode, 0)) - 1
        own_slot = whole(jnp.where(listed, slot, 0))
        prompt_slot = jnp.sum(
            jnp.where(shared == page_id, shared_slot, 0), axis=1, keepdims=True
        ) - 1
        prompt = jnp.broadcast_to(prompt_slot, row.shape) >= 0
        base = jnp.where(prompt_slot >= 0, prompt_slot, SHARED_PAGES + own_slot) * PAGE
        mine = (row >= PREFILL) & (row - PREFILL == owner)
        limit_ref[index : index + 1, :] = jnp.where(prompt | mine, bound - base, 0)


def attention_kernel(
    own_rows,
    core_ref,
    mine_ref,
    limit_ref,
    residual_ref,
    query_one,
    query_two,
    own_key,
    own_value,
    far_key,
    far_value,
    out_ref,
    carried_ref,
):
    @pl.when(pl.program_id(0) == 0)
    def _():
        carried_ref[...] = residual_ref[0].astype(jnp.float32)

    core = lax.axis_index("c")
    mine = 2 * lax.axis_index("z") + core
    sides = (mine, mine + 1 - 2 * core)
    query = jnp.concatenate(
        [query_one[:, :HEAD], query_one[:, HEAD:], query_two[:, :HEAD], query_two[:, HEAD:]], axis=0
    )
    keys = jnp.concatenate([own_key[...], far_key[...]], axis=0)
    values = jnp.concatenate([own_value[...], far_value[...]], axis=0)
    scores = lax.dot_general(
        keys, query, (((1,), (1,)), ((), ())), preferred_element_type=jnp.float32
    ) * (HEAD ** (-0.5))
    token = lax.broadcasted_iota(jnp.int32, (PAGE, ROWS), 0)
    fresh = lax.broadcasted_iota(jnp.int32, (FRESH_PAD, ROWS), 0)
    row = lax.broadcasted_iota(jnp.int32, (FRESH_PAD, ROWS), 1)
    seen = []
    for side in range(2):
        for page in range(OWN_PAGES):
            limit = limit_ref[pl.ds(side * OWN_PAGES + page, 1), :]
            seen.append((token < limit).astype(jnp.int32))
        key_row = sides[side] * own_rows + fresh
        before = jnp.where((key_row < PREFILL) & (key_row <= row), 1, 0)
        same = jnp.where(key_row == row, 1, 0)
        visible = jnp.where(row < PREFILL, before, same)
        seen.append(jnp.where(fresh < own_rows, visible, 0))
    seen = jnp.concatenate(seen, axis=0)
    seen = jnp.concatenate([seen] * 4, axis=1) > 0
    scores = jnp.where(seen, scores, NEG_FILL)
    peak = jnp.max(scores, axis=0, keepdims=True)
    exps = jnp.where(seen, jnp.exp(scores - peak), 0.0)
    total = jnp.sum(exps, axis=0, keepdims=True)
    mixed = lax.dot_general(
        values,
        exps.astype(jnp.bfloat16),
        (((0,), (0,)), ((), ())),
        preferred_element_type=jnp.float32,
    )
    line = lax.broadcasted_iota(jnp.int32, (STATS, ROWS), 0)
    for half in range(2):
        stats = jnp.zeros((STATS, ROWS), jnp.float32)
        for head in range(2):
            column = (2 * half + head) * ROWS
            out_ref[half, pl.ds(head * HEAD, HEAD), :] = mixed[:, column : column + ROWS].astype(
                jnp.bfloat16
            )
            sent = pieces(peak[:, column : column + ROWS]) + pieces(
                total[:, column : column + ROWS]
            )
            for index, value in enumerate(sent):
                stats = jnp.where(line == 6 * head + index, value, stats)
        out_ref[half, pl.ds(2 * HEAD, STATS), :] = stats.astype(jnp.bfloat16)


def attention(core, mine, own_rows, limits, residual, queries, own_kv, far_kv):
    kv_heads = own_kv.shape[1] // (2 * HEAD)
    chips = 2 * kv_heads
    width = residual.shape[2]

    def kv_spec(offset):
        return pl.BlockSpec((KEYS, HEAD), lambda j, core, mine: (0, offset + j))

    return pl.pallas_call(
        functools.partial(attention_kernel, own_rows),
        grid_spec=pltpu.PrefetchScalarGridSpec(
            num_scalar_prefetch=2,
            grid=(kv_heads,),
            in_specs=[
                pl.BlockSpec(limits.shape, lambda j, core, mine: (0, 0)),
                pl.BlockSpec((1, own_rows, width), lambda j, core, mine: (0, mine[0], 0)),
                pl.BlockSpec((ROWS, 2 * HEAD), lambda j, core, mine: (0, 4 * j + core[0])),
                pl.BlockSpec((ROWS, 2 * HEAD), lambda j, core, mine: (0, 4 * j + 2 + core[0])),
                kv_spec(0),
                kv_spec(kv_heads),
                kv_spec(0),
                kv_spec(kv_heads),
            ],
            out_specs=[
                pl.BlockSpec((2, 2 * HEAD + STATS, ROWS), lambda j, core, mine: (j, 0, 0)),
                pl.BlockSpec((own_rows, width), lambda j, core, mine: (0, 0)),
            ],
        ),
        out_shape=(
            jax.ShapeDtypeStruct((chips, 2 * HEAD + STATS, ROWS), jnp.bfloat16),
            jax.ShapeDtypeStruct((own_rows, width), jnp.float32),
        ),
        compiler_params=WIDE_LIMIT,
        name="attention",
    )(core, mine, limits, residual, queries, queries, own_kv, own_kv, far_kv, far_kv)


def combine_kernel(parts_ref, out_ref):
    chips = parts_ref.shape[0]
    for head in range(2):
        peaks = []
        totals = []
        for source in range(chips):
            stats = parts_ref[source, pl.ds(2 * HEAD, STATS), :].astype(jnp.float32)
            lines = [stats[6 * head + k : 6 * head + k + 1] for k in range(6)]
            peaks.append(lines[0] + lines[1] + lines[2])
            totals.append(lines[3] + lines[4] + lines[5])
        peak = peaks[0]
        for other in peaks[1:]:
            peak = jnp.maximum(peak, other)
        total = jnp.zeros_like(peak)
        mixed = jnp.zeros((HEAD, ROWS), jnp.float32)
        for source in range(chips):
            factor = jnp.exp(peaks[source] - peak)
            total = total + totals[source] * factor
            mixed = mixed + parts_ref[source, pl.ds(head * HEAD, HEAD), :].astype(jnp.float32) * factor
        attended = (mixed / total).T.astype(jnp.bfloat16)
        for copy in range(out_ref.shape[0]):
            out_ref[copy, :, head * HEAD : (head + 1) * HEAD] = attended


def combine(parts, copies):
    return pl.pallas_call(
        combine_kernel,
        out_shape=jax.ShapeDtypeStruct((copies, ROWS, 2 * HEAD), jnp.bfloat16),
        compiler_params=LIMIT,
        name="combine",
    )(parts)


def pack_kernel(
    lens_ref,
    offset_ref,
    table_ref,
    shared_ref,
    out_ref,
    gate_ref,
    up_ref,
    down_ref,
    pages_ref,
    fresh_ref,
    weights_ref,
    kv_ref,
    spread_ref,
    limit_ref,
):
    column = 0
    for source in (out_ref, gate_ref, up_ref):
        for row in range(0, source.shape[0], HEAD):
            width = source.shape[1]
            weights_ref[:, column : column + width] = source[row : row + HEAD, :]
            column += width
    for copy in range(spread_ref.shape[0]):
        spread_ref[copy] = down_ref[...]
    for page in range(OWN_PAGES):
        kv_ref[page * PAGE : (page + 1) * PAGE, :] = pages_ref[page]
    own_rows = fresh_ref.shape[0]
    rest = FRESH_PAD - own_rows
    fresh = fresh_ref[...]
    if rest:
        fresh = jnp.concatenate([fresh, jnp.zeros((rest, fresh.shape[1]), jnp.bfloat16)], axis=0)
    kv_ref[OWN_PAGES * PAGE :, :] = fresh
    core = lax.axis_index("c")
    mine = 2 * lax.axis_index("z") + core
    sides = (mine, mine + 1 - 2 * core)
    page_ids = [side * OWN_PAGES + page for side in sides for page in range(OWN_PAGES)]
    fill_limits(page_ids, lens_ref, offset_ref, table_ref, shared_ref, limit_ref)


def pack(copies, lens, offset, table, shared, weights, down_weight, pages, fresh):
    width = sum((piece.shape[0] // HEAD) * piece.shape[1] for piece in weights)
    smem = pl.BlockSpec(memory_space=pltpu.SMEM)
    vmem = pl.BlockSpec(memory_space=pltpu.VMEM)
    return pl.pallas_call(
        pack_kernel,
        in_specs=[smem] * 2 + [vmem] * 8,
        out_shape=(
            jax.ShapeDtypeStruct((HEAD, width), jnp.bfloat16),
            jax.ShapeDtypeStruct((KEYS, fresh.shape[1]), jnp.bfloat16),
            jax.ShapeDtypeStruct((copies,) + down_weight.shape, jnp.bfloat16),
            jax.ShapeDtypeStruct((2 * OWN_PAGES, ROWS), jnp.int32),
        ),
        compiler_params=WIDE_LIMIT,
        name="pack",
    )(lens, offset, table, shared, *weights, down_weight, pages, fresh)


def out_kernel(place_ref, attended_ref, weights_ref, *rest):
    result_ref = rest[-1]
    weights = jnp.concatenate([weights_ref[:, :HEAD], weights_ref[:, HEAD:]], axis=0)
    product = jnp.dot(attended_ref[...], weights, preferred_element_type=jnp.float32)
    if len(rest) == 2:
        product = product + rest[0][...].astype(jnp.float32)
    result_ref[...] = product.astype(jnp.bfloat16)


def out_product(half, attended, weights, far=None):
    rows = attended.shape[0]
    steps = weights.shape[0] // (2 * HEAD)
    column = pl.BlockSpec((rows, HEAD), lambda i, half: (0, i))
    return pl.pallas_call(
        out_kernel,
        grid_spec=pltpu.PrefetchScalarGridSpec(
            num_scalar_prefetch=1,
            grid=(steps,),
            in_specs=[
                pl.BlockSpec((rows, 2 * HEAD), lambda i, half: (0, 0)),
                pl.BlockSpec((HEAD, 2 * HEAD), lambda i, half: (half[0] * steps + i, 0)),
            ]
            + ([] if far is None else [column]),
            out_specs=column,
        ),
        out_shape=jax.ShapeDtypeStruct((rows, steps * HEAD), jnp.bfloat16),
        compiler_params=LIMIT,
        name="out_product",
    )(half, attended, weights, *(() if far is None else (far,)))


def norm_kernel(parts_ref, residual_ref, gain_ref, updated_ref, sent_ref):
    x_size, z_size = parts_ref.shape[:2]
    blocks = parts_ref.shape[4] // HEAD
    square = jnp.zeros((parts_ref.shape[3], 1), jnp.float32)
    for x in range(x_size):
        for core in range(2):
            summed = parts_ref[x, 0, core].astype(jnp.float32)
            for z in range(1, z_size):
                summed = summed + parts_ref[x, z, core].astype(jnp.float32)
            for block in range(blocks):
                column = ((core * blocks + block) * x_size + x) * HEAD
                value = summed[:, block * HEAD : (block + 1) * HEAD]
                value = value + residual_ref[:, column : column + HEAD]
                square = square + jnp.sum(value * value, axis=1, keepdims=True)
                updated_ref[:, column : column + HEAD] = value
    scale = lax.rsqrt(square / (2 * x_size * blocks * HEAD) + EPSILON)
    for x in range(x_size):
        for core in range(2):
            normed = []
            for block in range(blocks):
                column = ((core * blocks + block) * x_size + x) * HEAD
                value = updated_ref[:, column : column + HEAD] * scale
                normed.append(value * gain_ref[:, column : column + HEAD])
            normed = jnp.concatenate(normed, axis=1).astype(jnp.bfloat16)
            for z in range(z_size):
                sent_ref[x, z, core] = normed


def add_and_norm(parts, residual, gain):
    return pl.pallas_call(
        norm_kernel,
        out_shape=(
            jax.ShapeDtypeStruct(residual.shape, jnp.float32),
            jax.ShapeDtypeStruct(parts.shape, jnp.bfloat16),
        ),
        compiler_params=LIMIT,
        name="add_and_norm",
    )(parts, residual, gain.reshape(1, -1))


def gate_kernel(near_ref, far_ref, near_rows, far_rows, near_weights, far_weights, gated_ref):
    product = jnp.dot(near_rows[...], near_weights[...], preferred_element_type=jnp.float32)
    product = product + jnp.dot(
        far_rows[...], far_weights[...], preferred_element_type=jnp.float32
    )
    gated_ref[...] = product.astype(jnp.bfloat16)


def gate_product(near_half, far_half, near_rows, far_rows, weights):
    rows, depth = near_rows.shape
    tile = 2 * HEAD
    steps = weights.shape[1] // tile - 1
    whole = pl.BlockSpec((rows, depth), lambda i, near, far: (0, 0))
    return pl.pallas_call(
        gate_kernel,
        grid_spec=pltpu.PrefetchScalarGridSpec(
            num_scalar_prefetch=2,
            grid=(steps,),
            in_specs=[
                whole,
                whole,
                pl.BlockSpec((depth, tile), lambda i, near, far: (near[0], 1 + i)),
                pl.BlockSpec((depth, tile), lambda i, near, far: (far[0], 1 + i)),
            ],
            out_specs=pl.BlockSpec((rows, tile), lambda i, near, far: (0, i)),
        ),
        out_shape=jax.ShapeDtypeStruct((rows, steps * tile), jnp.bfloat16),
        compiler_params=LIMIT,
        name="gate_product",
    )(near_half, far_half, near_rows, far_rows, weights, weights)


def times_down(hidden, down_ref):
    blocks = jnp.concatenate([down_ref[block] for block in range(down_ref.shape[0])], axis=1)
    return jnp.dot(hidden, blocks, preferred_element_type=jnp.float32)


def hidden_kernel(half_ref, parts_ref, down_ref, hidden_ref, far_ref):
    @pl.when(pl.program_id(0) == 0)
    def _():
        summed = parts_ref[0].astype(jnp.float32)
        for source in range(1, parts_ref.shape[0]):
            summed = summed + parts_ref[source].astype(jnp.float32)
        units = summed.shape[1] // 2
        gate = summed[:, :units]
        hidden_ref[...] = (gate / (1.0 + jnp.exp(-gate)) * summed[:, units:]).astype(jnp.bfloat16)

    far_ref[...] = times_down(hidden_ref[...], down_ref).astype(jnp.bfloat16)


def down_spec(down, steps):
    blocks = down.shape[0] // (2 * steps)
    return pl.BlockSpec((blocks,) + down.shape[1:], lambda i, half: (half[0] * steps + i, 0, 0))


def hidden_product(half, parts, down):
    units = down.shape[1]
    steps = 4 if down.shape[0] % 8 == 0 else 1
    width = down.shape[0] // 2 * HEAD
    return pl.pallas_call(
        hidden_kernel,
        grid_spec=pltpu.PrefetchScalarGridSpec(
            num_scalar_prefetch=1,
            grid=(steps,),
            in_specs=[
                pl.BlockSpec(parts.shape, lambda i, half: (0, 0, 0)),
                down_spec(down, steps),
            ],
            out_specs=[
                pl.BlockSpec((ROWS, units), lambda i, half: (0, 0)),
                pl.BlockSpec((ROWS, width // steps), lambda i, half: (0, i)),
            ],
        ),
        out_shape=(
            jax.ShapeDtypeStruct((ROWS, units), jnp.bfloat16),
            jax.ShapeDtypeStruct((ROWS, width), jnp.bfloat16),
        ),
        compiler_params=LIMIT,
        name="hidden_product",
    )(half, parts, down)


def down_kernel(half_ref, hidden_ref, down_ref, far_ref, near_ref):
    product = times_down(hidden_ref[...], down_ref) + far_ref[...].astype(jnp.float32)
    near_ref[...] = product.astype(jnp.bfloat16)


def down_product(half, hidden, down, far):
    steps = 4 if down.shape[0] % 8 == 0 else 1
    column = pl.BlockSpec((ROWS, far.shape[1] // steps), lambda i, half: (0, i))
    return pl.pallas_call(
        down_kernel,
        grid_spec=pltpu.PrefetchScalarGridSpec(
            num_scalar_prefetch=1,
            grid=(steps,),
            in_specs=[
                pl.BlockSpec(hidden.shape, lambda i, half: (0, 0)),
                down_spec(down, steps),
                column,
            ],
            out_specs=column,
        ),
        out_shape=jax.ShapeDtypeStruct(far.shape, jnp.bfloat16),
        compiler_params=LIMIT,
        name="down_product",
    )(half, hidden, down, far)


def swap(value):
    return lax.ppermute(value, "c", [(0, 1), (1, 0)])


def local(
    queries,
    fresh_kv,
    kv_pages,
    residual,
    norm_gain,
    out_weight,
    gate_weight,
    up_weight,
    down_weight,
    page_table,
    shared_pages,
    cache_lens,
    prefill_offsets,
):
    y_size, x_size, z_size = lax.axis_size("y"), lax.axis_size("x"), lax.axis_size("z")
    core = lax.axis_index("c")
    mine = lax.axis_index("z") * 2 + core
    near_half, far_half = core.reshape(1), (1 - core).reshape(1)
    own_rows = fresh_kv.shape[1]
    half = y_size // 2

    packed, own_kv, spread, limits = pack(
        x_size,
        cache_lens,
        prefill_offsets,
        jnp.transpose(page_table, (2, 0, 1)),
        shared_pages,
        (out_weight, gate_weight, up_weight),
        down_weight,
        kv_pages[0],
        fresh_kv[0],
    )
    weights = lax.all_gather(packed, "y", axis=0, tiled=True)
    far_kv = swap(own_kv)
    down = lax.all_to_all(spread, "x", 0, 0, tiled=True)
    parts, carried = attention(
        near_half, mine.reshape(1), own_rows, limits, residual, queries[0], own_kv, far_kv
    )
    parts, down = lax.optimization_barrier((parts, down))
    down = lax.all_gather(down, "y", axis=0, tiled=True)
    parts = lax.all_to_all(parts, "z", 0, 0, tiled=True)
    attended = lax.all_to_all(combine(parts, x_size), "x", 0, 0, tiled=True)
    attended = attended.reshape(x_size * ROWS, 2 * HEAD)

    columns = weights[:, : 2 * HEAD]
    far = swap(out_product(far_half, attended, columns))
    parts = out_product(near_half, attended, columns, far)
    parts = lax.all_to_all(parts, ("x", "z", "c"), 0, 0, tiled=True)
    parts = parts.reshape(x_size, z_size, 2, own_rows, half * HEAD)
    updated, sent = add_and_norm(parts, carried, norm_gain)
    near_rows = lax.all_to_all(
        sent.reshape(x_size * ROWS, half * HEAD), ("x", "z", "c"), 0, 0, tiled=True
    )
    far_rows, down = lax.optimization_barrier((swap(near_rows), down))

    gated = gate_product(near_half, far_half, near_rows, far_rows, weights)
    gated = lax.all_to_all(gated, "x", 0, 0, tiled=True)
    gated = gated.reshape(x_size, ROWS, gated.shape[1])
    hidden, far = hidden_product(far_half, gated, down)
    parts = down_product(near_half, hidden, down, swap(far))
    parts = lax.all_to_all(parts, ("z", "c"), 0, 0, tiled=True)
    parts = parts.reshape(z_size, 2, own_rows, parts.shape[1])
    returned = jnp.transpose(jnp.sum(parts.astype(jnp.float32), axis=0), (1, 0, 2))
    return (updated + returned.reshape(own_rows, -1)).astype(jnp.bfloat16)[None]


def solution(mesh):
    cores = 2
    chips = mesh.shape["mlp"] // cores
    along = 4 if mesh.shape["grp"] % 16 == 0 else 2
    long_mesh = Mesh(
        mesh.devices.reshape(mesh.shape["grp"] // along, along, chips, cores), LONG
    )
    grp, mlp = ("y", "x"), ("z", "c")
    placed = (
        P(grp, None, None),
        P(grp, mlp, None),
        P(grp, mlp, None, None),
        P(grp, None, None),
        P(),
        P(mlp, grp),
        P(grp, mlp),
        P(grp, mlp),
        P(mlp, grp),
        P(grp, None, None),
        P(grp, None),
        P(grp, None),
        P(grp),
    )
    return jax.shard_map(
        local, mesh=long_mesh, in_specs=placed, out_specs=P(grp, mlp, None), check_vma=False
    )
```

```python
import functools

import jax
import jax.numpy as jnp
from jax import lax
from jax.experimental import pallas as pl
from jax.experimental.pallas import tpu as pltpu
from jax.sharding import Mesh
from jax.sharding import PartitionSpec as P

HEAD = 128
PAGE = 128
SHARED_PAGES = 4
PRIVATE_PAGES = 12
DECODES = 16
PREFILL = 112
ROWS = 128
OWN_PAGES = 2
FRESH_PAD = 16
KEYS = OWN_PAGES * PAGE + FRESH_PAD
STATS = 16
NEG_FILL = -1e30
EPSILON = 1e-05
LONG = "y", "x", "z", "c"
LIMIT = pltpu.CompilerParams(vmem_limit_bytes=32 * 1024 * 1024)
WIDE_LIMIT = pltpu.CompilerParams(vmem_limit_bytes=60 * 1024 * 1024)


def pieces(value):
    first = value.astype(jnp.bfloat16).astype(jnp.float32)
    rest = value - first
    second = rest.astype(jnp.bfloat16).astype(jnp.float32)
    return (first, second, rest - second)


def fill_limits(page_ids, lens_ref, offset_ref, table_ref, shared_ref, limit_ref):
    row = lax.broadcasted_iota(jnp.int32, (1, ROWS), 1)
    bound = jnp.full((1, ROWS), offset_ref[0], jnp.int32)
    for decode in range(DECODES):
        bound = jnp.where(row == PREFILL + decode, lens_ref[0, decode], bound)
    table, shared = table_ref[...], shared_ref[...]
    slot = lax.broadcasted_iota(jnp.int32, table.shape, 0)
    decode = lax.broadcasted_iota(jnp.int32, table.shape, 2) + 1
    shared_slot = lax.broadcasted_iota(jnp.int32, shared.shape, 1) + 1

    def whole(values):
        return jnp.sum(jnp.sum(values, axis=0), axis=1, keepdims=True)

    for index, page_id in enumerate(page_ids):
        listed = table == page_id
        owner = whole(jnp.where(listed, decode, 0)) - 1
        own_slot = whole(jnp.where(listed, slot, 0))
        prompt_slot = jnp.sum(
            jnp.where(shared == page_id, shared_slot, 0), axis=1, keepdims=True
        ) - 1
        prompt = jnp.broadcast_to(prompt_slot, row.shape) >= 0
        base = jnp.where(prompt_slot >= 0, prompt_slot, SHARED_PAGES + own_slot) * PAGE
        mine = (row >= PREFILL) & (row - PREFILL == owner)
        limit_ref[index : index + 1, :] = jnp.where(prompt | mine, bound - base, 0)


def attention_kernel(
    own_rows,
    core_ref,
    mine_ref,
    limit_ref,
    residual_ref,
    query_one,
    query_two,
    own_key,
    own_value,
    far_key,
    far_value,
    out_ref,
    carried_ref,
):
    @pl.when(pl.program_id(0) == 0)
    def _():
        carried_ref[...] = residual_ref[0].astype(jnp.float32)

    core = lax.axis_index("c")
    mine = 2 * lax.axis_index("z") + core
    sides = (mine, mine + 1 - 2 * core)
    query = jnp.concatenate(
        [query_one[:, :HEAD], query_one[:, HEAD:], query_two[:, :HEAD], query_two[:, HEAD:]], axis=0
    )
    keys = jnp.concatenate([own_key[...], far_key[...]], axis=0)
    values = jnp.concatenate([own_value[...], far_value[...]], axis=0)
    scores = lax.dot_general(
        keys, query, (((1,), (1,)), ((), ())), preferred_element_type=jnp.float32
    ) * (HEAD ** (-0.5))
    token = lax.broadcasted_iota(jnp.int32, (PAGE, ROWS), 0)
    fresh = lax.broadcasted_iota(jnp.int32, (FRESH_PAD, ROWS), 0)
    row = lax.broadcasted_iota(jnp.int32, (FRESH_PAD, ROWS), 1)
    seen = []
    for side in range(2):
        for page in range(OWN_PAGES):
            limit = limit_ref[pl.ds(side * OWN_PAGES + page, 1), :]
            seen.append((token < limit).astype(jnp.int32))
        key_row = sides[side] * own_rows + fresh
        before = jnp.where((key_row < PREFILL) & (key_row <= row), 1, 0)
        same = jnp.where(key_row == row, 1, 0)
        visible = jnp.where(row < PREFILL, before, same)
        seen.append(jnp.where(fresh < own_rows, visible, 0))
    seen = jnp.concatenate(seen, axis=0)
    seen = jnp.concatenate([seen] * 4, axis=1) > 0
    scores = jnp.where(seen, scores, NEG_FILL)
    peak = jnp.max(scores, axis=0, keepdims=True)
    exps = jnp.where(seen, jnp.exp(scores - peak), 0.0)
    total = jnp.sum(exps, axis=0, keepdims=True)
    mixed = lax.dot_general(
        values,
        exps.astype(jnp.bfloat16),
        (((0,), (0,)), ((), ())),
        preferred_element_type=jnp.float32,
    )
    line = lax.broadcasted_iota(jnp.int32, (STATS, ROWS), 0)
    for half in range(2):
        stats = jnp.zeros((STATS, ROWS), jnp.float32)
        for head in range(2):
            column = (2 * half + head) * ROWS
            out_ref[half, pl.ds(head * HEAD, HEAD), :] = mixed[:, column : column + ROWS].astype(
                jnp.bfloat16
            )
            sent = pieces(peak[:, column : column + ROWS]) + pieces(
                total[:, column : column + ROWS]
            )
            for index, value in enumerate(sent):
                stats = jnp.where(line == 6 * head + index, value, stats)
        out_ref[half, pl.ds(2 * HEAD, STATS), :] = stats.astype(jnp.bfloat16)


def attention(core, mine, own_rows, limits, residual, queries, own_kv, far_kv):
    kv_heads = own_kv.shape[1] // (2 * HEAD)
    chips = 2 * kv_heads
    width = residual.shape[2]

    def kv_spec(offset):
        return pl.BlockSpec((KEYS, HEAD), lambda j, core, mine: (0, offset + j))

    return pl.pallas_call(
        functools.partial(attention_kernel, own_rows),
        grid_spec=pltpu.PrefetchScalarGridSpec(
            num_scalar_prefetch=2,
            grid=(kv_heads,),
            in_specs=[
                pl.BlockSpec(limits.shape, lambda j, core, mine: (0, 0)),
                pl.BlockSpec((1, own_rows, width), lambda j, core, mine: (0, mine[0], 0)),
                pl.BlockSpec((ROWS, 2 * HEAD), lambda j, core, mine: (0, 4 * j + core[0])),
                pl.BlockSpec((ROWS, 2 * HEAD), lambda j, core, mine: (0, 4 * j + 2 + core[0])),
                kv_spec(0),
                kv_spec(kv_heads),
                kv_spec(0),
                kv_spec(kv_heads),
            ],
            out_specs=[
                pl.BlockSpec((2, 2 * HEAD + STATS, ROWS), lambda j, core, mine: (j, 0, 0)),
                pl.BlockSpec((own_rows, width), lambda j, core, mine: (0, 0)),
            ],
        ),
        out_shape=(
            jax.ShapeDtypeStruct((chips, 2 * HEAD + STATS, ROWS), jnp.bfloat16),
            jax.ShapeDtypeStruct((own_rows, width), jnp.float32),
        ),
        compiler_params=WIDE_LIMIT,
        name="attention",
    )(core, mine, limits, residual, queries, queries, own_kv, own_kv, far_kv, far_kv)


def combine_kernel(parts_ref, out_ref):
    chips = parts_ref.shape[0]
    for head in range(2):
        peaks = []
        totals = []
        for source in range(chips):
            stats = parts_ref[source, pl.ds(2 * HEAD, STATS), :].astype(jnp.float32)
            lines = [stats[6 * head + k : 6 * head + k + 1] for k in range(6)]
            peaks.append(lines[0] + lines[1] + lines[2])
            totals.append(lines[3] + lines[4] + lines[5])
        peak = peaks[0]
        for other in peaks[1:]:
            peak = jnp.maximum(peak, other)
        total = jnp.zeros_like(peak)
        mixed = jnp.zeros((HEAD, ROWS), jnp.float32)
        for source in range(chips):
            factor = jnp.exp(peaks[source] - peak)
            total = total + totals[source] * factor
            mixed = mixed + parts_ref[source, pl.ds(head * HEAD, HEAD), :].astype(jnp.float32) * factor
        attended = (mixed / total).T.astype(jnp.bfloat16)
        for copy in range(out_ref.shape[0]):
            out_ref[copy, :, head * HEAD : (head + 1) * HEAD] = attended


def combine(parts, copies):
    return pl.pallas_call(
        combine_kernel,
        out_shape=jax.ShapeDtypeStruct((copies, ROWS, 2 * HEAD), jnp.bfloat16),
        compiler_params=LIMIT,
        name="combine",
    )(parts)


def pack_kernel(
    lens_ref,
    offset_ref,
    table_ref,
    shared_ref,
    out_ref,
    gate_ref,
    up_ref,
    down_ref,
    pages_ref,
    fresh_ref,
    weights_ref,
    kv_ref,
    spread_ref,
    limit_ref,
):
    column = 0
    for source in (out_ref, gate_ref, up_ref):
        for row in range(0, source.shape[0], HEAD):
            width = source.shape[1]
            weights_ref[:, column : column + width] = source[row : row + HEAD, :]
            column += width
    for copy in range(spread_ref.shape[0]):
        spread_ref[copy] = down_ref[...]
    for page in range(OWN_PAGES):
        kv_ref[page * PAGE : (page + 1) * PAGE, :] = pages_ref[page]
    own_rows = fresh_ref.shape[0]
    rest = FRESH_PAD - own_rows
    fresh = fresh_ref[...]
    if rest:
        fresh = jnp.concatenate([fresh, jnp.zeros((rest, fresh.shape[1]), jnp.bfloat16)], axis=0)
    kv_ref[OWN_PAGES * PAGE :, :] = fresh
    core = lax.axis_index("c")
    mine = 2 * lax.axis_index("z") + core
    sides = (mine, mine + 1 - 2 * core)
    page_ids = [side * OWN_PAGES + page for side in sides for page in range(OWN_PAGES)]
    fill_limits(page_ids, lens_ref, offset_ref, table_ref, shared_ref, limit_ref)


def pack(copies, lens, offset, table, shared, weights, down_weight, pages, fresh):
    width = sum((piece.shape[0] // HEAD) * piece.shape[1] for piece in weights)
    smem = pl.BlockSpec(memory_space=pltpu.SMEM)
    vmem = pl.BlockSpec(memory_space=pltpu.VMEM)
    return pl.pallas_call(
        pack_kernel,
        in_specs=[smem] * 2 + [vmem] * 8,
        out_shape=(
            jax.ShapeDtypeStruct((HEAD, width), jnp.bfloat16),
            jax.ShapeDtypeStruct((KEYS, fresh.shape[1]), jnp.bfloat16),
            jax.ShapeDtypeStruct((copies,) + down_weight.shape, jnp.bfloat16),
            jax.ShapeDtypeStruct((2 * OWN_PAGES, ROWS), jnp.int32),
        ),
        compiler_params=WIDE_LIMIT,
        name="pack",
    )(lens, offset, table, shared, *weights, down_weight, pages, fresh)


def out_kernel(place_ref, attended_ref, weights_ref, *rest):
    result_ref = rest[-1]
    weights = jnp.concatenate([weights_ref[:, :HEAD], weights_ref[:, HEAD:]], axis=0)
    product = jnp.dot(attended_ref[...], weights, preferred_element_type=jnp.float32)
    if len(rest) == 2:
        product = product + rest[0][...].astype(jnp.float32)
    result_ref[...] = product.astype(jnp.bfloat16)


def out_product(half, attended, weights, far=None):
    rows = attended.shape[0]
    steps = weights.shape[0] // (2 * HEAD)
    column = pl.BlockSpec((rows, HEAD), lambda i, half: (0, i))
    return pl.pallas_call(
        out_kernel,
        grid_spec=pltpu.PrefetchScalarGridSpec(
            num_scalar_prefetch=1,
            grid=(steps,),
            in_specs=[
                pl.BlockSpec((rows, 2 * HEAD), lambda i, half: (0, 0)),
                pl.BlockSpec((HEAD, 2 * HEAD), lambda i, half: (half[0] * steps + i, 0)),
            ]
            + ([] if far is None else [column]),
            out_specs=column,
        ),
        out_shape=jax.ShapeDtypeStruct((rows, steps * HEAD), jnp.bfloat16),
        compiler_params=LIMIT,
        name="out_product",
    )(half, attended, weights, *(() if far is None else (far,)))


def norm_kernel(parts_ref, residual_ref, gain_ref, updated_ref, sent_ref):
    x_size, z_size = parts_ref.shape[:2]
    blocks = parts_ref.shape[4] // HEAD
    square = jnp.zeros((parts_ref.shape[3], 1), jnp.float32)
    for x in range(x_size):
        for core in range(2):
            summed = parts_ref[x, 0, core].astype(jnp.float32)
            for z in range(1, z_size):
                summed = summed + parts_ref[x, z, core].astype(jnp.float32)
            for block in range(blocks):
                column = ((core * blocks + block) * x_size + x) * HEAD
                value = summed[:, block * HEAD : (block + 1) * HEAD]
                value = value + residual_ref[:, column : column + HEAD]
                square = square + jnp.sum(value * value, axis=1, keepdims=True)
                updated_ref[:, column : column + HEAD] = value
    scale = lax.rsqrt(square / (2 * x_size * blocks * HEAD) + EPSILON)
    for x in range(x_size):
        for core in range(2):
            normed = []
            for block in range(blocks):
                column = ((core * blocks + block) * x_size + x) * HEAD
                value = updated_ref[:, column : column + HEAD] * scale
                normed.append(value * gain_ref[:, column : column + HEAD])
            normed = jnp.concatenate(normed, axis=1).astype(jnp.bfloat16)
            for z in range(z_size):
                sent_ref[x, z, core] = normed


def add_and_norm(parts, residual, gain):
    return pl.pallas_call(
        norm_kernel,
        out_shape=(
            jax.ShapeDtypeStruct(residual.shape, jnp.float32),
            jax.ShapeDtypeStruct(parts.shape, jnp.bfloat16),
        ),
        compiler_params=LIMIT,
        name="add_and_norm",
    )(parts, residual, gain.reshape(1, -1))


def gate_kernel(near_ref, far_ref, near_rows, far_rows, near_weights, far_weights, gated_ref):
    product = jnp.dot(near_rows[...], near_weights[...], preferred_element_type=jnp.float32)
    product = product + jnp.dot(
        far_rows[...], far_weights[...], preferred_element_type=jnp.float32
    )
    gated_ref[...] = product.astype(jnp.bfloat16)


def gate_product(near_half, far_half, near_rows, far_rows, weights):
    rows, depth = near_rows.shape
    tile = 2 * HEAD
    steps = weights.shape[1] // tile - 1
    whole = pl.BlockSpec((rows, depth), lambda i, near, far: (0, 0))
    return pl.pallas_call(
        gate_kernel,
        grid_spec=pltpu.PrefetchScalarGridSpec(
            num_scalar_prefetch=2,
            grid=(steps,),
            in_specs=[
                whole,
                whole,
                pl.BlockSpec((depth, tile), lambda i, near, far: (near[0], 1 + i)),
                pl.BlockSpec((depth, tile), lambda i, near, far: (far[0], 1 + i)),
            ],
            out_specs=pl.BlockSpec((rows, tile), lambda i, near, far: (0, i)),
        ),
        out_shape=jax.ShapeDtypeStruct((rows, steps * tile), jnp.bfloat16),
        compiler_params=LIMIT,
        name="gate_product",
    )(near_half, far_half, near_rows, far_rows, weights, weights)


def times_down(hidden, down_ref):
    return jnp.concatenate(
        [
            jnp.dot(hidden, down_ref[block], preferred_element_type=jnp.float32)
            for block in range(down_ref.shape[0])
        ],
        axis=1,
    )


def hidden_kernel(half_ref, parts_ref, down_ref, hidden_ref, far_ref):
    @pl.when(pl.program_id(0) == 0)
    def _():
        summed = parts_ref[0].astype(jnp.float32)
        for source in range(1, parts_ref.shape[0]):
            summed = summed + parts_ref[source].astype(jnp.float32)
        units = summed.shape[1] // 2
        gate = summed[:, :units]
        hidden_ref[...] = (gate / (1.0 + jnp.exp(-gate)) * summed[:, units:]).astype(jnp.bfloat16)

    far_ref[...] = times_down(hidden_ref[...], down_ref).astype(jnp.bfloat16)


def down_spec(down, steps):
    blocks = down.shape[0] // (2 * steps)
    return pl.BlockSpec((blocks,) + down.shape[1:], lambda i, half: (half[0] * steps + i, 0, 0))


def hidden_product(half, parts, down):
    units = down.shape[1]
    steps = 2 if down.shape[0] % 8 == 0 else 1
    width = down.shape[0] // 2 * HEAD
    return pl.pallas_call(
        hidden_kernel,
        grid_spec=pltpu.PrefetchScalarGridSpec(
            num_scalar_prefetch=1,
            grid=(steps,),
            in_specs=[
                pl.BlockSpec(parts.shape, lambda i, half: (0, 0, 0)),
                down_spec(down, steps),
            ],
            out_specs=[
                pl.BlockSpec((ROWS, units), lambda i, half: (0, 0)),
                pl.BlockSpec((ROWS, width // steps), lambda i, half: (0, i)),
            ],
        ),
        out_shape=(
            jax.ShapeDtypeStruct((ROWS, units), jnp.bfloat16),
            jax.ShapeDtypeStruct((ROWS, width), jnp.bfloat16),
        ),
        compiler_params=LIMIT,
        name="hidden_product",
    )(half, parts, down)


def down_kernel(half_ref, hidden_ref, down_ref, far_ref, near_ref):
    product = times_down(hidden_ref[...], down_ref) + far_ref[...].astype(jnp.float32)
    near_ref[...] = product.astype(jnp.bfloat16)


def down_product(half, hidden, down, far):
    steps = 2 if down.shape[0] % 8 == 0 else 1
    column = pl.BlockSpec((ROWS, far.shape[1] // steps), lambda i, half: (0, i))
    return pl.pallas_call(
        down_kernel,
        grid_spec=pltpu.PrefetchScalarGridSpec(
            num_scalar_prefetch=1,
            grid=(steps,),
            in_specs=[
                pl.BlockSpec(hidden.shape, lambda i, half: (0, 0)),
                down_spec(down, steps),
                column,
            ],
            out_specs=column,
        ),
        out_shape=jax.ShapeDtypeStruct(far.shape, jnp.bfloat16),
        compiler_params=LIMIT,
        name="down_product",
    )(half, hidden, down, far)


def swap(value):
    return lax.ppermute(value, "c", [(0, 1), (1, 0)])


def local(
    queries,
    fresh_kv,
    kv_pages,
    residual,
    norm_gain,
    out_weight,
    gate_weight,
    up_weight,
    down_weight,
    page_table,
    shared_pages,
    cache_lens,
    prefill_offsets,
):
    y_size, x_size, z_size = lax.axis_size("y"), lax.axis_size("x"), lax.axis_size("z")
    core = lax.axis_index("c")
    mine = lax.axis_index("z") * 2 + core
    near_half, far_half = core.reshape(1), (1 - core).reshape(1)
    own_rows = fresh_kv.shape[1]
    half = y_size // 2

    packed, own_kv, spread, limits = pack(
        x_size,
        cache_lens,
        prefill_offsets,
        jnp.transpose(page_table, (2, 0, 1)),
        shared_pages,
        (out_weight, gate_weight, up_weight),
        down_weight,
        kv_pages[0],
        fresh_kv[0],
    )
    weights = lax.all_gather(packed, "y", axis=0, tiled=True)
    far_kv = swap(own_kv)
    down = lax.all_to_all(spread, "x", 0, 0, tiled=True)
    parts, carried = attention(
        near_half, mine.reshape(1), own_rows, limits, residual, queries[0], own_kv, far_kv
    )
    parts, down = lax.optimization_barrier((parts, down))
    parts = lax.all_to_all(parts, "z", 0, 0, tiled=True)
    combined = combine(parts, x_size)
    down, _ = lax.optimization_barrier((down, combined))
    down = lax.all_gather(down, "y", axis=0, tiled=True)
    attended = lax.all_to_all(combined, "x", 0, 0, tiled=True)
    attended = attended.reshape(x_size * ROWS, 2 * HEAD)

    columns = weights[:, : 2 * HEAD]
    far = swap(out_product(far_half, attended, columns))
    parts = out_product(near_half, attended, columns, far)
    parts = lax.all_to_all(parts, ("x", "z", "c"), 0, 0, tiled=True)
    parts = parts.reshape(x_size, z_size, 2, own_rows, half * HEAD)
    updated, sent = add_and_norm(parts, carried, norm_gain)
    near_rows = lax.all_to_all(
        sent.reshape(x_size * ROWS, half * HEAD), ("x", "z", "c"), 0, 0, tiled=True
    )
    far_rows, down = lax.optimization_barrier((swap(near_rows), down))

    gated = gate_product(near_half, far_half, near_rows, far_rows, weights)
    gated = lax.all_to_all(gated, "x", 0, 0, tiled=True)
    gated = gated.reshape(x_size, ROWS, gated.shape[1])
    hidden, far = hidden_product(far_half, gated, down)
    parts = down_product(near_half, hidden, down, swap(far))
    parts = lax.all_to_all(parts, ("z", "c"), 0, 0, tiled=True)
    parts = parts.reshape(z_size, 2, own_rows, parts.shape[1])
    returned = jnp.transpose(jnp.sum(parts.astype(jnp.float32), axis=0), (1, 0, 2))
    return (updated + returned.reshape(own_rows, -1)).astype(jnp.bfloat16)[None]


def solution(mesh):
    cores = 2
    chips = mesh.shape["mlp"] // cores
    along = 4 if mesh.shape["grp"] % 16 == 0 else 2
    long_mesh = Mesh(
        mesh.devices.reshape(mesh.shape["grp"] // along, along, chips, cores), LONG
    )
    grp, mlp = ("y", "x"), ("z", "c")
    placed = (
        P(grp, None, None),
        P(grp, mlp, None),
        P(grp, mlp, None, None),
        P(grp, None, None),
        P(),
        P(mlp, grp),
        P(grp, mlp),
        P(grp, mlp),
        P(mlp, grp),
        P(grp, None, None),
        P(grp, None),
        P(grp, None),
        P(grp),
    )
    return jax.shard_map(
        local, mesh=long_mesh, in_specs=placed, out_specs=P(grp, mlp, None), check_vma=False
    )
```
